32 devices in a mesh: ctx: 8 (over y, x, core), dp: 4 (over z).
Axes of the slice: x: 2, y: 2, z: 4, core: 2. Of those that a mesh axis runs over, the one named last changes fastest.
Arguments:
- tokens: bfloat16 [4, 1024, 1536], P('dp', 'ctx'), may hold values from -6 to 6
- w_in: bfloat16 [1536, 2880], replicated, may hold values from -0.15625 to 0.15625
- conv_taps: float32 [7, 2880], replicated, may hold values from -2.4 to 2.4
- residues: float32 [960, 16], P('ctx'), may hold values from -1.5 to 1.5
- rates: float32 [960, 16], P('ctx'), may hold values from 0.00029296875 to 0.08
- cotangent: bfloat16 [4, 1024, 960], P('dp', 'ctx'), may hold values from -6 to 6
Outputs:
- output: bfloat16 [4, 1024, 960], P('dp', 'ctx')
- grad_tokens: bfloat16 [4, 1024, 1536], P('dp', 'ctx')
- grad_weight: bfloat16 [1536, 2880], P('ctx', 'dp')
- grad_taps: float32 [7, 2880], replicated
- grad_residues: float32 [960, 16], P('ctx')
The draws below stay inside these ranges and needn't reach their ends.
All inputs are finite; a program needn't handle non-finite values.
Results may differ from the reference program's by a relative error of at most 0.02.
Values may be sent and summed in bfloat16 or wider, within the bound.
A program may use at most 192 MiB of HBM per device.

```python
import math
import jax
import jax.numpy as jnp
from jax import lax

D = 1536
CH = 960
ORDER = 16
TAPS = 7
SEQ_LEN = 1024
SEQS = 4
C = 2880


def draw_rates(key, part):
    key = jax.random.fold_in(key, 11)
    key_pick, key_slow, key_fast = jax.random.split(key, 3)
    share = 0.5
    pick = jax.random.uniform(key_pick, (CH, ORDER), jnp.float32) < share
    slow = jnp.exp(jax.random.uniform(key_slow, (CH, ORDER), jnp.float32, jnp.log(0.3 / SEQ_LEN), jnp.log(2.0 / SEQ_LEN)))
    fast = jnp.exp(jax.random.uniform(key_fast, (CH, ORDER), jnp.float32, jnp.log(0.02), jnp.log(0.08)))
    return jnp.where(pick, slow, fast).astype(jnp.float32)


def shard_levels(key, extent, pieces, low, top_value):
    def one(dim, blocks):
        heights = jax.random.uniform(jax.random.fold_in(jax.random.fold_in(key, 6), dim), (blocks,), jnp.float32, low / len(pieces), top_value / len(pieces))
        return jnp.repeat(jnp.exp(heights), extent[dim] // blocks).reshape((-1,) + (1,) * (len(extent) - dim - 1))

    level = one(*pieces[0])
    for cut in pieces[1:]:
        level = level * one(*cut)
    return level


def bell_draw(key, dims, scale, most, cuts=(), held_as=jnp.bfloat16):
    entries = jax.random.normal(key, dims, jnp.float32) * scale
    if len(cuts) > 0:
        entries = shard_levels(key, dims, cuts, -0.22, 0.18) * entries
    return jnp.clip(entries, min=-most, max=most).astype(held_as)


def setup_inputs(seed: int = 0) -> dict:
    keys = jax.random.split(jax.random.key(seed), 7)
    tokens = bell_draw(keys[0], (SEQS, SEQ_LEN, D), 1.0, 6.0, ((0, 4), (1, 8)))
    w_in = bell_draw(keys[1], (D, C), D ** -0.5, 0.15625)
    conv_taps = bell_draw(keys[2], (TAPS, C), 0.4, 2.4, (), jnp.float32)
    residues = bell_draw(keys[3], (CH, ORDER), 0.25, 1.5, ((0, 8),), jnp.float32)
    rates = draw_rates(jax.random.fold_in(keys[6], 71), 0)
    cotangent = bell_draw(keys[5], (SEQS, SEQ_LEN, CH), 1.0, 6.0, ((0, 4), (1, 8)))
    return {"tokens": tokens, "w_in": w_in, "conv_taps": conv_taps, "residues": residues, "rates": rates, "cotangent": cotangent}


def reference(tokens, w_in, conv_taps, residues, rates, cotangent):
    scale = 1.0 / math.sqrt(SEQS * SEQ_LEN)
    flat = tokens.reshape(-1, D)
    z = jnp.dot(flat, w_in, preferred_element_type=jnp.float32).astype(jnp.bfloat16)
    z = z.reshape(SEQS, SEQ_LEN, 3 * CH)
    zpad = jnp.pad(z, ((0, 0), (TAPS - 1, 0), (0, 0)))
    mixed = jnp.zeros((SEQS, SEQ_LEN, 3 * CH), jnp.float32)
    for j in range(TAPS):
        mixed = mixed + conv_taps[j] * zpad[:, TAPS - 1 - j:TAPS - 1 - j + SEQ_LEN].astype(jnp.float32)
    query = mixed[..., :CH]
    keyed = mixed[..., CH:2 * CH]
    valued = mixed[..., 2 * CH:]
    product = (keyed * valued).astype(jnp.bfloat16)
    amp = jnp.sqrt(-jnp.expm1(-2.0 * rates))
    reff = residues * amp
    steps = jnp.arange(SEQ_LEN).astype(jnp.float32)
    filt = jnp.zeros((CH, SEQ_LEN), jnp.float32)
    for k in range(ORDER):
        filt = filt + reff[:, k, None] * jnp.exp(-rates[:, k, None] * steps)
    filt_f = jnp.fft.rfft(filt, n=2 * SEQ_LEN)

    def conv_one(seq):
        spec_seq = jnp.fft.rfft(seq.T, n=2 * SEQ_LEN)
        return jnp.fft.irfft(spec_seq * filt_f, n=2 * SEQ_LEN)[:, :SEQ_LEN].T
    long_out = lax.map(conv_one, product.astype(jnp.float32)).astype(jnp.bfloat16)
    output = (query * long_out.astype(jnp.float32)).astype(jnp.bfloat16)
    upstream = cotangent.astype(jnp.float32)
    dquery = upstream * long_out.astype(jnp.float32)
    dlong = (upstream * query).astype(jnp.bfloat16)

    def back_one(seq):
        return jnp.flip(conv_one(jnp.flip(seq, 0)), 0)
    dproduct = lax.map(back_one, dlong.astype(jnp.float32)).astype(jnp.bfloat16)

    def corr_one(pair):
        left = jnp.fft.rfft(pair[0].T, n=2 * SEQ_LEN)
        right = jnp.fft.rfft(pair[1].T, n=2 * SEQ_LEN)
        return jnp.fft.irfft(jnp.conj(left) * right, n=2 * SEQ_LEN)[:, :SEQ_LEN]
    corr = lax.optimization_barrier(jnp.sum(lax.map(corr_one, (product.astype(jnp.float32), dlong.astype(jnp.float32))), axis=0))
    columns = []
    for k in range(ORDER):
        columns.append(lax.optimization_barrier(jnp.sum(corr * jnp.exp(-rates[:, k, None] * steps), axis=1)))
    grad_residues = amp * jnp.stack(columns, axis=1) * scale
    dprod32 = dproduct.astype(jnp.float32)
    dmixed = jnp.concatenate([dquery, dprod32 * valued, dprod32 * keyed], axis=-1).astype(jnp.bfloat16)
    dm32 = dmixed.astype(jnp.float32)
    tap_rows = []
    for j in range(TAPS):
        tap_rows.append(lax.optimization_barrier(jnp.sum(dm32 * zpad[:, TAPS - 1 - j:TAPS - 1 - j + SEQ_LEN].astype(jnp.float32), axis=(0, 1))))
    grad_taps = jnp.stack(tap_rows, axis=0) * scale
    dpad = jnp.pad(dmixed, ((0, 0), (0, TAPS - 1), (0, 0)))
    dz = jnp.zeros((SEQS, SEQ_LEN, 3 * CH), jnp.float32)
    for j in range(TAPS):
        dz = dz + conv_taps[j] * dpad[:, j:j + SEQ_LEN].astype(jnp.float32)
    dz = dz.astype(jnp.bfloat16).reshape(-1, 3 * CH)
    grad_tokens = jnp.dot(dz, w_in.T, preferred_element_type=jnp.float32).astype(jnp.bfloat16)
    grad_tokens = grad_tokens.reshape(SEQS, SEQ_LEN, D)
    grad_weight = (jnp.dot(flat.T, dz, preferred_element_type=jnp.float32) * scale).astype(jnp.bfloat16)
    return (output, grad_tokens, grad_weight, grad_taps, grad_residues)
```

```python
import functools
import math

import jax
import jax.numpy as jnp
from jax import lax
from jax.experimental import pallas as pl
from jax.experimental.pallas import tpu as pltpu
from jax.sharding import PartitionSpec as P

LANES = 128
SUB = 8
HALO = 16
GROUP = 32

VM = pl.BlockSpec(memory_space=pltpu.VMEM)
SM = pl.BlockSpec(memory_space=pltpu.SMEM)
PARAMS = pltpu.CompilerParams(vmem_limit_bytes=48 << 20)
f32 = jnp.float32
bf16 = jnp.bfloat16


def lane_tiles(width):
    return [(a, min(a + LANES, width)) for a in range(0, width, LANES)]


def sub_index(first, sign, lanes):
    rows = lax.broadcasted_iota(jnp.int32, (SUB, lanes), 0).astype(f32)
    return first + sign * rows


def fold_down(rate, load, blocks, first, sign, order):
    ratio = jnp.exp(-float(SUB) * rate)
    total = None
    for a in order(blocks):
        block = load(a)
        total = block if total is None else total * ratio + block
    weight = jnp.exp(-rate * sub_index(first, sign, rate.shape[1]))
    return jnp.sum(total * weight, axis=0, keepdims=True)


def forwards(blocks):
    return list(range(blocks))


def backwards(blocks):
    return list(range(blocks - 1, -1, -1))


def states_kernel(width, z_ref, taps_ref, cot_ref, rate_ref, qkv_ref, up_ref, gp_ref, eh_ref, zs, mixed):
    rows = cot_ref.shape[0]
    count = taps_ref.shape[0]
    modes, wide = rate_ref.shape
    blocks = rows // SUB
    for a, b in lane_tiles(z_ref.shape[1]):
        zs[:, a:b] = z_ref[:, a:b].astype(f32)
        total = jnp.zeros((rows, b - a), f32)
        for j in range(count):
            total = total + taps_ref[j : j + 1, a:b] * zs[HALO - j : HALO - j + rows, a:b]
        mixed[:, a:b] = total
    if wide > width:
        for part in range(3):
            qkv_ref[part, :, width:] = jnp.zeros((rows, wide - width), f32)
        up_ref[:, width:] = jnp.zeros((2 * rows, wide - width), f32)
        gp_ref[:, width:] = jnp.zeros((2 * rows, wide - width), f32)
    up_ref[:rows, :width] = jnp.zeros((rows, width), f32)
    gp_ref[rows:, :width] = jnp.zeros((rows, width), f32)
    for part in range(3):
        qkv_ref[part, :, :width] = mixed[:, part * width : (part + 1) * width]
    for a, b in lane_tiles(width):
        product = (qkv_ref[1, :, a:b] * qkv_ref[2, :, a:b]).astype(bf16)
        up_ref[rows:, a:b] = product.astype(f32)
        dlong = (cot_ref[:, a:b].astype(f32) * qkv_ref[0, :, a:b]).astype(bf16)
        gp_ref[:rows, a:b] = dlong.astype(f32)
    for a, b in lane_tiles(wide):
        for k in range(modes):
            rate = rate_ref[k : k + 1, a:b]
            eh_ref[k : k + 1, a:b] = fold_down(
                rate, lambda i: up_ref[rows + i * SUB : rows + (i + 1) * SUB, a:b],
                blocks, float(SUB - 1), -1.0, forwards)
            eh_ref[modes + k : modes + k + 1, a:b] = fold_down(
                rate, lambda i: gp_ref[i * SUB : (i + 1) * SUB, a:b], blocks, 0.0, 1.0, backwards)


def spread_modes(rate_ref, coef, ref, lanes, first, sign, order, blocks):
    modes = rate_ref.shape[0]
    totals = [ref[i * SUB : (i + 1) * SUB, lanes] for i in range(blocks)]
    for k in range(modes):
        rate = rate_ref[k : k + 1, lanes]
        ratio = jnp.exp(-float(SUB) * rate)
        term = coef(k) * jnp.exp(-rate * sub_index(first, sign, LANES))
        steps = order(blocks)
        for i in steps:
            totals[i] = totals[i] + term
            if i != steps[-1]:
                term = term * ratio
    for i in range(blocks):
        ref[i * SUB : (i + 1) * SUB, lanes] = totals[i]


def near_kernel(up_ref, gp_ref, rate_ref, reff_ref, inf_ref, inb_ref, near_ref, filt, corr, ups, gps):
    rows = inf_ref.shape[0]
    modes, wide = rate_ref.shape
    blocks = rows // SUB
    inf_ref[...] = jnp.zeros((rows, wide), f32)
    inb_ref[...] = jnp.zeros((rows, wide), f32)
    filt[...] = jnp.zeros((rows, wide), f32)
    index = lax.broadcasted_iota(jnp.int32, (SUB, LANES), 0)

    @pl.loop(0, wide // LANES)
    def _(tile):
        lanes = pl.ds(pl.multiple_of(tile * LANES, LANES), LANES)
        spread_modes(rate_ref, lambda k: reff_ref[k : k + 1, lanes], filt, lanes, 0.0, 1.0, forwards, blocks)
        for s in range(SUB):
            ups[s, SUB:, :] = up_ref[SUB - s : 2 * rows - s, lanes]
            gps[s, : 2 * rows - SUB, :] = gp_ref[s : 2 * rows - SUB + s, lanes]
        for low in range(0, rows, GROUP):
            size = rows - low

            def body(step, carry):
                acc_f, acc_b = carry
                base = pl.multiple_of(low + step * SUB, SUB)
                taps = filt[pl.ds(base, SUB), lanes]
                lags = jnp.zeros((SUB, LANES), f32)
                for s in range(SUB):
                    tap = taps[s : s + 1]
                    moved = ups[s, pl.ds(pl.multiple_of(rows + low - base, SUB), size), :]
                    acc_f = acc_f + tap * moved
                    pair = jnp.sum(gp_ref[low:rows, lanes] * moved, axis=0, keepdims=True)
                    lags = jnp.where(index == s, pair, lags)
                    acc_b = acc_b + tap * gps[s, pl.ds(base, size), :]
                corr[pl.ds(base, SUB), lanes] = lags
                return acc_f, acc_b

            acc_f, acc_b = lax.fori_loop(
                0, GROUP // SUB, body, (inf_ref[low:rows, lanes], inb_ref[0:size, lanes]))
            inf_ref[low:rows, lanes] = acc_f
            inb_ref[0:size, lanes] = acc_b
        for k in range(modes):
            near_ref[k : k + 1, lanes] = fold_down(
                rate_ref[k : k + 1, lanes], lambda i: corr[i * SUB : (i + 1) * SUB, lanes],
                blocks, 0.0, 1.0, backwards)


def join_kernel(width, me_ref, qkv_ref, inf_ref, inb_ref, near_ref, cot_ref, rate_ref, reff_ref, all_ref, z_ref,
                out_ref, dm_ref, tap_ref, draw_ref, first, last, lf, lb, dm, zs):
    rows = cot_ref.shape[0]
    modes, wide = rate_ref.shape
    blocks = rows // SUB
    devices = all_ref.shape[0]
    count = tap_ref.shape[0]
    me = me_ref[0]
    rate = rate_ref[...]
    first[...] = jnp.zeros((modes, wide), f32)
    last[...] = jnp.zeros((modes, wide), f32)

    @pl.loop(0, devices)
    def _(d):
        ahead = jnp.maximum(me - 1 - d, 0).astype(f32)
        keep = jnp.where(d < me, 1.0, 0.0)
        first[...] += keep * jnp.exp(-rate * (ahead * float(rows))) * all_ref[d, 0:modes]
        behind = jnp.maximum(d - me - 1, 0).astype(f32)
        hold = jnp.where(d > me, 1.0, 0.0)
        last[...] += hold * jnp.exp(-rate * (behind * float(rows))) * all_ref[d, modes : 2 * modes]

    draw_ref[...] = near_ref[...] + first[...] * all_ref[me, modes : 2 * modes] * jnp.exp(-rate)
    first[...] = first[...] * reff_ref[...]
    last[...] = last[...] * reff_ref[...]
    lf[...] = inf_ref[...]
    lb[...] = inb_ref[...]

    @pl.loop(0, wide // LANES)
    def _(tile):
        lanes = pl.ds(pl.multiple_of(tile * LANES, LANES), LANES)
        spread_modes(rate_ref, lambda k: first[k : k + 1, lanes], lf, lanes, 1.0, 1.0, forwards, blocks)
        spread_modes(rate_ref, lambda k: last[k : k + 1, lanes], lb, lanes, float(SUB), -1.0, backwards, blocks)

    for a, b in lane_tiles(width):
        far = lf[:, a:b].astype(bf16).astype(f32)
        out_ref[:, a:b] = (qkv_ref[0, :, a:b] * far).astype(bf16)
        lf[:, a:b] = cot_ref[:, a:b].astype(f32) * far
        lb[:, a:b] = lb[:, a:b].astype(bf16).astype(f32)
    dm[:, 0:width] = lf[:, 0:width]
    dm[:, width : 2 * width] = lb[:, 0:width] * qkv_ref[2, :, 0:width]
    dm[:, 2 * width : 3 * width] = lb[:, 0:width] * qkv_ref[1, :, 0:width]
    for a, b in lane_tiles(3 * width):
        held = dm[:, a:b].astype(bf16)
        dm_ref[:, a:b] = held
        held = held.astype(f32)
        zs[:, a:b] = z_ref[:, a:b].astype(f32)
        for j in range(count):
            tap_ref[j : j + 1, a:b] = jnp.sum(
                held * zs[HALO - j : HALO - j + rows, a:b], axis=0, keepdims=True)


def dz_kernel(dm_ref, after_ref, taps_ref, dz_ref, cut_ref, pad, full):
    rows = dm_ref.shape[0]
    parts, _, piece = cut_ref.shape
    count = taps_ref.shape[0]
    for a, b in lane_tiles(dm_ref.shape[1]):
        pad[0:rows, a:b] = dm_ref[:, a:b].astype(f32)
        pad[rows:, a:b] = after_ref[:, a:b].astype(f32)
        total = jnp.zeros((rows, b - a), f32)
        for j in range(count):
            total = total + taps_ref[j : j + 1, a:b] * pad[j : j + rows, a:b]
        dz_ref[:, a:b] = total.astype(bf16)
        full[:, a:b] = total
    for p in range(parts):
        cut_ref[p] = full[:, p * piece : (p + 1) * piece].astype(bf16)


def shape(dims, kind=f32):
    return jax.ShapeDtypeStruct(dims, kind)


def call(kernel, outs, scratch, ops, scalars=0, flops=10**8):
    return pl.pallas_call(
        kernel,
        out_shape=outs,
        in_specs=[SM] * scalars + [VM] * (len(ops) - scalars),
        out_specs=[VM] * len(outs),
        scratch_shapes=[pltpu.VMEM(dims, f32) for dims in scratch],
        compiler_params=PARAMS,
        cost_estimate=pl.CostEstimate(flops=flops, bytes_accessed=1 << 22, transcendentals=0),
    )(*ops)


def shifted(block, axis, distance):
    devices = range(lax.axis_size(axis))
    route = [(i - distance, i) for i in devices if i - distance in devices]
    return lax.ppermute(block, axis, route)


def local(tokens, w_in, conv_taps, residues, rates, cotangent):
    feats = tokens[0]
    rows, depth = feats.shape
    cot = cotangent[0]
    width = cot.shape[1]
    chans = w_in.shape[1]
    own, modes = rates.shape
    count = conv_taps.shape[0]
    ctx = lax.axis_size("ctx")
    dp = lax.axis_size("dp")
    me = lax.axis_index("ctx")
    scale = 1.0 / math.sqrt(dp * ctx * rows)
    wide = -(-width // LANES) * LANES

    amp = jnp.sqrt(-jnp.expm1(-2.0 * rates))
    modal = jnp.concatenate([rates.T, (residues * amp).T], axis=0)
    modal = lax.all_gather(modal, "ctx", axis=0, tiled=False)
    modal = modal.transpose(1, 0, 2).reshape(2 * modes, width)
    modal = jnp.pad(modal, ((0, 0), (0, wide - width)))
    rate_t, reff_t = modal[:modes], modal[modes:]

    before = shifted(feats[rows - HALO :], "ctx", 1)
    stacked = jnp.concatenate([before, feats], axis=0)
    z = jnp.dot(stacked, w_in, preferred_element_type=f32).astype(bf16)

    qkv, up, gp, eh = call(
        functools.partial(states_kernel, width),
        [shape((3, rows, wide)), shape((2 * rows, wide)), shape((2 * rows, wide)), shape((2 * modes, wide))],
        [(HALO + rows, chans), (rows, chans)],
        (z, conv_taps, cot, rate_t))
    every = lax.all_gather(eh, "ctx", axis=0, tiled=False)
    inner_f, inner_b, near = call(
        near_kernel,
        [shape((rows, wide)), shape((rows, wide)), shape((modes, wide))],
        [(rows, wide), (rows, wide), (SUB, 2 * rows, LANES), (SUB, 2 * rows, LANES)],
        (up, gp, rate_t, reff_t), flops=5 * 10**9)
    output, dmixed, tap_part, draw = call(
        functools.partial(join_kernel, width),
        [shape((rows, width), bf16), shape((rows, chans), bf16), shape((count, chans)), shape((modes, wide))],
        [(modes, wide), (modes, wide), (rows, wide), (rows, wide), (rows, chans), (HALO + rows, chans)],
        (me.reshape(1), qkv, inner_f, inner_b, near, cot, rate_t, reff_t, every, z), scalars=1)

    after = shifted(dmixed[:HALO], "ctx", -1)
    dz, cut = call(
        dz_kernel,
        [shape((rows, chans), bf16), shape((dp, rows, chans // dp), bf16)],
        [(rows + HALO, chans), (rows, chans)],
        (dmixed, after, conv_taps))

    feats_all = lax.all_gather(feats, "dp", axis=0, tiled=True)
    swapped = lax.all_to_all(cut, "dp", split_axis=0, concat_axis=0, tiled=True)
    grad_feats = lax.dot_general(
        dz, w_in, (((1,), (1,)), ((), ())), preferred_element_type=f32).astype(bf16)
    term = lax.dot_general(
        feats_all, swapped.reshape(dp * rows, chans // dp), (((0,), (0,)), ((), ())),
        preferred_element_type=f32).astype(bf16)
    arrived = lax.all_to_all(
        term.reshape(ctx, depth // ctx, chans // dp), "ctx", split_axis=0, concat_axis=0, tiled=True)
    grad_weight = (jnp.sum(arrived.astype(f32), axis=0) * scale).astype(bf16)

    tap_sum, draw_sum = lax.psum((tap_part, draw[:, :width]), ("ctx", "dp"))
    grad_taps = tap_sum * scale
    mine = lax.dynamic_slice_in_dim(draw_sum, me * own, own, axis=1)
    grad_residues = amp * mine.T * scale
    return (output[None], grad_feats[None], grad_weight, grad_taps, grad_residues)


def solution(mesh):
    in_specs = (
        P("dp", "ctx", None),
        P(),
        P(),
        P("ctx", None),
        P("ctx", None),
        P("dp", "ctx", None),
    )
    out_specs = (P("dp", "ctx", None), P("dp", "ctx", None), P("ctx", "dp"), P(), P("ctx", None))
    return jax.shard_map(local, mesh=mesh, in_specs=in_specs, out_specs=out_specs, check_vma=False)
```

```python
import functools
import math

import jax
import jax.numpy as jnp
from jax import lax
from jax.experimental import pallas as pl
from jax.experimental.pallas import tpu as pltpu
from jax.sharding import PartitionSpec as P

LANES = 128
SUB = 8
HALO = 16
GROUP = 32

VM = pl.BlockSpec(memory_space=pltpu.VMEM)
SM = pl.BlockSpec(memory_space=pltpu.SMEM)
PARAMS = pltpu.CompilerParams(vmem_limit_bytes=48 << 20)
f32 = jnp.float32
bf16 = jnp.bfloat16


def lane_tiles(width):
    return [(a, min(a + LANES, width)) for a in range(0, width, LANES)]


def sub_index(first, sign, lanes):
    rows = lax.broadcasted_iota(jnp.int32, (SUB, lanes), 0).astype(f32)
    return first + sign * rows


def fold_down(rate, load, blocks, first, sign, order):
    ratio = jnp.exp(-float(SUB) * rate)
    total = None
    for a in order(blocks):
        block = load(a)
        total = block if total is None else total * ratio + block
    weight = jnp.exp(-rate * sub_index(first, sign, rate.shape[1]))
    return jnp.sum(total * weight, axis=0, keepdims=True)


def forwards(blocks):
    return list(range(blocks))


def backwards(blocks):
    return list(range(blocks - 1, -1, -1))


def states_kernel(width, z_ref, taps_ref, cot_ref, rate_ref, qkv_ref, up_ref, gp_ref, eh_ref, zs, mixed):
    rows = cot_ref.shape[0]
    count = taps_ref.shape[0]
    modes, wide = rate_ref.shape
    blocks = rows // SUB
    for a, b in lane_tiles(z_ref.shape[1]):
        zs[:, a:b] = z_ref[:, a:b].astype(f32)
        total = jnp.zeros((rows, b - a), f32)
        for j in range(count):
            total = total + taps_ref[j : j + 1, a:b] * zs[HALO - j : HALO - j + rows, a:b]
        mixed[:, a:b] = total
    if wide > width:
        for part in range(3):
            qkv_ref[part, :, width:] = jnp.zeros((rows, wide - width), f32)
        up_ref[:, width:] = jnp.zeros((2 * rows, wide - width), f32)
        gp_ref[:, width:] = jnp.zeros((2 * rows, wide - width), f32)
    up_ref[:rows, :width] = jnp.zeros((rows, width), f32)
    gp_ref[rows:, :width] = jnp.zeros((rows, width), f32)
    for part in range(3):
        qkv_ref[part, :, :width] = mixed[:, part * width : (part + 1) * width]
    for a, b in lane_tiles(width):
        product = (qkv_ref[1, :, a:b] * qkv_ref[2, :, a:b]).astype(bf16)
        up_ref[rows:, a:b] = product.astype(f32)
        dlong = (cot_ref[:, a:b].astype(f32) * qkv_ref[0, :, a:b]).astype(bf16)
        gp_ref[:rows, a:b] = dlong.astype(f32)
    for a, b in lane_tiles(wide):
        for k in range(modes):
            rate = rate_ref[k : k + 1, a:b]
            eh_ref[k : k + 1, a:b] = fold_down(
                rate, lambda i: up_ref[rows + i * SUB : rows + (i + 1) * SUB, a:b],
                blocks, float(SUB - 1), -1.0, forwards)
            eh_ref[modes + k : modes + k + 1, a:b] = fold_down(
                rate, lambda i: gp_ref[i * SUB : (i + 1) * SUB, a:b], blocks, 0.0, 1.0, backwards)


def spread_modes(rate_ref, coef, ref, lanes, first, sign, order, blocks):
    modes = rate_ref.shape[0]
    totals = [ref[i * SUB : (i + 1) * SUB, lanes] for i in range(blocks)]
    for k in range(modes):
        rate = rate_ref[k : k + 1, lanes]
        ratio = jnp.exp(-float(SUB) * rate)
        term = coef(k) * jnp.exp(-rate * sub_index(first, sign, LANES))
        steps = order(blocks)
        for i in steps:
            totals[i] = totals[i] + term
            if i != steps[-1]:
                term = term * ratio
    for i in range(blocks):
        ref[i * SUB : (i + 1) * SUB, lanes] = totals[i]


def near_kernel(up_ref, gp_ref, rate_ref, reff_ref, inf_ref, inb_ref, near_ref, filt, corr, ups, gps):
    rows = inf_ref.shape[0]
    modes, wide = rate_ref.shape
    blocks = rows // SUB
    inf_ref[...] = jnp.zeros((rows, wide), f32)
    inb_ref[...] = jnp.zeros((rows, wide), f32)
    filt[...] = jnp.zeros((rows, wide), f32)
    index = lax.broadcasted_iota(jnp.int32, (SUB, LANES), 0)

    @pl.loop(0, wide // LANES)
    def _(tile):
        lanes = pl.ds(pl.multiple_of(tile * LANES, LANES), LANES)
        spread_modes(rate_ref, lambda k: reff_ref[k : k + 1, lanes], filt, lanes, 0.0, 1.0, forwards, blocks)
        for s in range(SUB):
            ups[s, SUB:, :] = up_ref[SUB - s : 2 * rows - s, lanes]
            gps[s, : 2 * rows - SUB, :] = gp_ref[s : 2 * rows - SUB + s, lanes]
        for low in range(0, rows, GROUP):
            size = rows - low

            def body(step, carry):
                acc_f, acc_b = carry
                base = pl.multiple_of(low + step * SUB, SUB)
                taps = filt[pl.ds(base, SUB), lanes]
                lags = jnp.zeros((SUB, LANES), f32)
                for s in range(SUB):
                    tap = taps[s : s + 1]
                    moved = ups[s, pl.ds(pl.multiple_of(rows + low - base, SUB), size), :]
                    acc_f = acc_f + tap * moved
                    pair = jnp.sum(gp_ref[low:rows, lanes] * moved, axis=0, keepdims=True)
                    lags = jnp.where(index == s, pair, lags)
                    acc_b = acc_b + tap * gps[s, pl.ds(base, size), :]
                corr[pl.ds(base, SUB), lanes] = lags
                return acc_f, acc_b

            acc_f, acc_b = lax.fori_loop(
                0, GROUP // SUB, body, (inf_ref[low:rows, lanes], inb_ref[0:size, lanes]))
            inf_ref[low:rows, lanes] = acc_f
            inb_ref[0:size, lanes] = acc_b
        for k in range(modes):
            near_ref[k : k + 1, lanes] = fold_down(
                rate_ref[k : k + 1, lanes], lambda i: corr[i * SUB : (i + 1) * SUB, lanes],
                blocks, 0.0, 1.0, backwards)


def join_kernel(width, me_ref, qkv_ref, inf_ref, inb_ref, near_ref, cot_ref, rate_ref, reff_ref, all_ref, z_ref,
                out_ref, dm_ref, stat_ref, first, last, lf, lb, dm, zs, tap_ref, draw_ref):
    rows = cot_ref.shape[0]
    modes, wide = rate_ref.shape
    blocks = rows // SUB
    devices = all_ref.shape[0]
    count = tap_ref.shape[0] - 1
    me = me_ref[0]
    rate = rate_ref[...]
    first[...] = jnp.zeros((modes, wide), f32)
    last[...] = jnp.zeros((modes, wide), f32)

    @pl.loop(0, devices)
    def _(d):
        ahead = jnp.maximum(me - 1 - d, 0).astype(f32)
        keep = jnp.where(d < me, 1.0, 0.0)
        first[...] += keep * jnp.exp(-rate * (ahead * float(rows))) * all_ref[d, 0:modes]
        behind = jnp.maximum(d - me - 1, 0).astype(f32)
        hold = jnp.where(d > me, 1.0, 0.0)
        last[...] += hold * jnp.exp(-rate * (behind * float(rows))) * all_ref[d, modes : 2 * modes]

    draw_ref[...] = near_ref[...] + first[...] * all_ref[me, modes : 2 * modes] * jnp.exp(-rate)
    first[...] = first[...] * reff_ref[...]
    last[...] = last[...] * reff_ref[...]
    lf[...] = inf_ref[...]
    lb[...] = inb_ref[...]

    @pl.loop(0, wide // LANES)
    def _(tile):
        lanes = pl.ds(pl.multiple_of(tile * LANES, LANES), LANES)
        spread_modes(rate_ref, lambda k: first[k : k + 1, lanes], lf, lanes, 1.0, 1.0, forwards, blocks)
        spread_modes(rate_ref, lambda k: last[k : k + 1, lanes], lb, lanes, float(SUB), -1.0, backwards, blocks)

    for a, b in lane_tiles(width):
        far = lf[:, a:b].astype(bf16).astype(f32)
        out_ref[:, a:b] = (qkv_ref[0, :, a:b] * far).astype(bf16)
        lf[:, a:b] = cot_ref[:, a:b].astype(f32) * far
        lb[:, a:b] = lb[:, a:b].astype(bf16).astype(f32)
    dm[:, 0:width] = lf[:, 0:width]
    dm[:, width : 2 * width] = lb[:, 0:width] * qkv_ref[2, :, 0:width]
    dm[:, 2 * width : 3 * width] = lb[:, 0:width] * qkv_ref[1, :, 0:width]
    for a, b in lane_tiles(3 * width):
        held = dm[:, a:b].astype(bf16)
        dm_ref[:, a:b] = held
        held = held.astype(f32)
        zs[:, a:b] = z_ref[:, a:b].astype(f32)
        for j in range(count):
            tap_ref[j : j + 1, a:b] = jnp.sum(
                held * zs[HALO - j : HALO - j + rows, a:b], axis=0, keepdims=True)
    stat_ref[...] = jnp.zeros(stat_ref.shape, f32)
    cols = 3 * width // devices
    own = width // devices
    for d in range(devices):
        stat_ref[d, 0:count, :] = tap_ref[0:count, d * cols : (d + 1) * cols]
        stat_ref[d, SUB : SUB + modes, 0:own] = draw_ref[:, d * own : (d + 1) * own]


def dz_kernel(dm_ref, after_ref, taps_ref, dz_ref, cut_ref, pad, full):
    rows = dm_ref.shape[0]
    parts, _, piece = cut_ref.shape
    count = taps_ref.shape[0]
    for a, b in lane_tiles(dm_ref.shape[1]):
        pad[0:rows, a:b] = dm_ref[:, a:b].astype(f32)
        pad[rows:, a:b] = after_ref[:, a:b].astype(f32)
        total = jnp.zeros((rows, b - a), f32)
        for j in range(count):
            total = total + taps_ref[j : j + 1, a:b] * pad[j : j + rows, a:b]
        dz_ref[:, a:b] = total.astype(bf16)
        full[:, a:b] = total
    for p in range(parts):
        cut_ref[p] = full[:, p * piece : (p + 1) * piece].astype(bf16)


def others(axis):
    size = lax.axis_size(axis)
    me = lax.axis_index(axis)
    return [lax.rem(me + j, size) for j in range(1, size)]


def greet(axes):
    barrier = pltpu.get_barrier_semaphore()
    count = 0
    for axis in axes:
        for peer in others(axis):
            pl.semaphore_signal(barrier, inc=1, device_id={axis: peer}, device_id_type=pl.DeviceIdType.MESH)
            count += 1
    pl.semaphore_wait(barrier, count)


def push(axis, peer, src, dst, send, recv):
    return pltpu.make_async_remote_copy(
        src_ref=src, dst_ref=dst, send_sem=send.at[peer], recv_sem=recv.at[lax.axis_index(axis)],
        device_id={axis: peer}, device_id_type=pl.DeviceIdType.MESH)


def arrival(axis, peer, src, dst, send, recv):
    return pltpu.make_async_remote_copy(
        src_ref=src, dst_ref=dst, send_sem=send.at[peer], recv_sem=recv.at[peer],
        device_id={axis: peer}, device_id_type=pl.DeviceIdType.MESH)


def start_kernel(feats_ref, modal_ref, halo_ref, all_ref, send, recv, hop_send, hop_recv):
    me = lax.axis_index("ctx")
    size = lax.axis_size("ctx")
    rows = feats_ref.shape[0]
    greet(["ctx"])
    hop = pltpu.make_async_remote_copy(
        src_ref=feats_ref.at[pl.ds(rows - HALO, HALO)], dst_ref=halo_ref, send_sem=hop_send, recv_sem=hop_recv,
        device_id={"ctx": lax.rem(me + 1, size)}, device_id_type=pl.DeviceIdType.MESH)
    hop.start()
    sent = [push("ctx", p, modal_ref, all_ref.at[me], send, recv) for p in others("ctx")]
    for copy in sent:
        copy.start()
    all_ref[me] = modal_ref[...]
    hop.wait()

    @pl.when(me == 0)
    def _():
        halo_ref[...] = jnp.zeros(halo_ref.shape, halo_ref.dtype)

    for p in others("ctx"):
        arrival("ctx", p, modal_ref, all_ref.at[p], send, recv).wait_recv()
    for copy in sent:
        copy.wait_send()


def inner_kernel(up_ref, gp_ref, rate_ref, reff_ref, eh_ref, turned_ref, inf_ref, inb_ref, near_ref, all_ref, toks_ref,
                 filt, corr, ups, gps, send, recv, tok_send, tok_recv):
    me = lax.axis_index("ctx")
    mine = lax.axis_index("dp")
    rows = turned_ref.shape[1]

    def slot(p):
        return toks_ref.at[:, pl.ds(pl.multiple_of(p * rows, rows), rows)]

    greet(["ctx", "dp"])
    sent = [push("ctx", p, eh_ref, all_ref.at[me], send, recv) for p in others("ctx")]
    for copy in sent:
        copy.start()
    swaps = [push("dp", p, turned_ref, slot(mine), tok_send, tok_recv) for p in others("dp")]
    for copy in swaps:
        copy.start()
    all_ref[me] = eh_ref[...]
    toks_ref[:, pl.ds(pl.multiple_of(mine * rows, rows), rows)] = turned_ref[...]
    near_kernel(up_ref, gp_ref, rate_ref, reff_ref, inf_ref, inb_ref, near_ref, filt, corr, ups, gps)
    for p in others("ctx"):
        arrival("ctx", p, eh_ref, all_ref.at[p], send, recv).wait_recv()
    for p in others("dp"):
        arrival("dp", p, turned_ref, slot(p), tok_send, tok_recv).wait_recv()
    for copy in sent + swaps:
        copy.wait_send()


def tokens_kernel(dz_ref, cut_ref, stat_ref, w_ref, got_ref, feats_ref, red_ref,
                  w_held, parts, column, rest, w_sem, cut_send, cut_recv, st_send, st_recv, col_send, col_recv):
    me = lax.axis_index("ctx")
    mine = lax.axis_index("dp")
    load = pltpu.make_async_copy(w_ref, w_held, w_sem)
    load.start()
    greet(["ctx", "dp"])
    sent = [push("ctx", p, stat_ref.at[p], parts.at[me], st_send, st_recv) for p in others("ctx")]
    for copy in sent:
        copy.start()
    swaps = [push("dp", p, cut_ref.at[p], got_ref.at[mine], cut_send, cut_recv) for p in others("dp")]
    for copy in swaps:
        copy.start()
    got_ref[mine] = cut_ref[mine]
    total = stat_ref[me]
    for p in others("ctx"):
        arrival("ctx", p, stat_ref.at[p], parts.at[p], st_send, st_recv).wait_recv()
        total = total + parts[p]
    column[...] = total
    spread = [push("dp", p, column, rest.at[mine], col_send, col_recv) for p in others("dp")]
    for copy in spread:
        copy.start()
    load.wait()
    tile = 2 * LANES

    @pl.loop(0, w_held.shape[0] // tile)
    def _(i):
        at = pl.ds(pl.multiple_of(i * tile, tile), tile)
        feats_ref[:, at] = lax.dot_general(
            dz_ref[...], w_held[at, :], (((1,), (1,)), ((), ())), preferred_element_type=f32).astype(bf16)

    rest[mine] = column[...]
    for p in others("dp"):
        arrival("dp", p, column, rest.at[p], col_send, col_recv).wait_recv()
    total = rest[0]
    for p in range(1, rest.shape[0]):
        total = total + rest[p]
    red_ref[...] = total
    for p in others("dp"):
        arrival("dp", p, cut_ref.at[p], got_ref.at[p], cut_send, cut_recv).wait_recv()
    for copy in sent + swaps + spread:
        copy.wait_send()


def weight_kernel(scale, toks_ref, got_ref, red_ref, gw_ref, taps_ref, term, land, total, send, recv, tap_send, tap_recv):
    me = lax.axis_index("ctx")
    devices, own, _ = term.shape
    per = 16 // math.gcd(own, 16)
    count = devices // per
    greet(["ctx"])
    sent = [push("ctx", p, red_ref, taps_ref.at[me], tap_send, tap_recv) for p in others("ctx")]
    for copy in sent:
        copy.start()
    taps_ref[me] = red_ref[...]

    @pl.loop(0, count)
    def _(i):
        block = lax.rem(me // per + 1 + i, count)
        at = pl.ds(pl.multiple_of(block * (own * per), 16), own * per)
        piece = jnp.dot(toks_ref[at, :], got_ref[...], preferred_element_type=f32)
        for s in range(per):
            target = block * per + s
            term[target] = piece[s * own : (s + 1) * own].astype(bf16)

            @pl.when(target != me)
            def _():
                push("ctx", target, term.at[target], land.at[me], send, recv).start()

    total[...] = term[me].astype(f32)
    for p in others("ctx"):
        arrival("ctx", p, term.at[p], land.at[p], send, recv).wait_recv()
        total[...] += land[p].astype(f32)
    gw_ref[...] = (total[...] * scale).astype(bf16)
    for p in others("ctx"):
        arrival("ctx", p, red_ref, taps_ref.at[p], tap_send, tap_recv).wait_recv()
        arrival("ctx", p, term.at[p], land.at[p], send, recv).wait_send()
    for copy in sent:
        copy.wait_send()


def shape(dims, kind=f32):
    return jax.ShapeDtypeStruct(dims, kind)


def call(kernel, outs, scratch, ops, scalars=0, flops=10**8):
    return pl.pallas_call(
        kernel,
        out_shape=outs,
        in_specs=[SM] * scalars + [VM] * (len(ops) - scalars),
        out_specs=[VM] * len(outs),
        scratch_shapes=[pltpu.VMEM(dims, f32) for dims in scratch],
        compiler_params=PARAMS,
        cost_estimate=pl.CostEstimate(flops=flops, bytes_accessed=1 << 22, transcendentals=0),
    )(*ops)


def exchange(kernel, number, outs, scratch, ops, anywhere=(), flops=10**8):
    specs = [pl.BlockSpec(memory_space=pl.ANY) if i in anywhere else VM for i in range(len(ops))]
    return pl.pallas_call(
        kernel,
        out_shape=outs,
        in_specs=specs,
        out_specs=[VM] * len(outs),
        scratch_shapes=scratch,
        compiler_params=pltpu.CompilerParams(
            vmem_limit_bytes=48 << 20, collective_id=number, has_side_effects=True),
        cost_estimate=pl.CostEstimate(flops=flops, bytes_accessed=1 << 22, transcendentals=0),
    )(*ops)


def shifted(block, axis, distance):
    devices = range(lax.axis_size(axis))
    route = [(i - distance, i) for i in devices if i - distance in devices]
    return lax.ppermute(block, axis, route)


def local(tokens, w_in, conv_taps, residues, rates, cotangent):
    feats = tokens[0]
    rows, depth = feats.shape
    cot = cotangent[0]
    width = cot.shape[1]
    chans = w_in.shape[1]
    own, modes = rates.shape
    count = conv_taps.shape[0]
    ctx = lax.axis_size("ctx")
    dp = lax.axis_size("dp")
    me = lax.axis_index("ctx")
    scale = 1.0 / math.sqrt(dp * ctx * rows)
    wide = -(-width // LANES) * LANES

    amp = jnp.sqrt(-jnp.expm1(-2.0 * rates))
    dma = pltpu.SemaphoreType.DMA
    modal = jnp.concatenate([rates.T, (residues * amp).T], axis=0)
    before, modal = exchange(
        start_kernel, 0,
        [shape((HALO, depth), bf16), shape((ctx, 2 * modes, own))],
        [dma((ctx,)), dma((ctx,)), dma, dma],
        (feats, modal))
    modal = modal.transpose(1, 0, 2).reshape(2 * modes, width)
    modal = jnp.pad(modal, ((0, 0), (0, wide - width)))
    rate_t, reff_t = modal[:modes], modal[modes:]

    stacked = jnp.concatenate([before, feats], axis=0)
    z = jnp.dot(stacked, w_in, preferred_element_type=f32).astype(bf16)

    qkv, up, gp, eh = call(
        functools.partial(states_kernel, width),
        [shape((3, rows, wide)), shape((2 * rows, wide)), shape((2 * rows, wide)), shape((2 * modes, wide))],
        [(HALO + rows, chans), (rows, chans)],
        (z, conv_taps, cot, rate_t))
    inner_f, inner_b, near, every, toks = exchange(
        inner_kernel, 1,
        [shape((rows, wide)), shape((rows, wide)), shape((modes, wide)), shape((ctx, 2 * modes, wide)),
         shape((depth, dp * rows), bf16)],
        [pltpu.VMEM((rows, wide), f32), pltpu.VMEM((rows, wide), f32),
         pltpu.VMEM((SUB, 2 * rows, LANES), f32), pltpu.VMEM((SUB, 2 * rows, LANES), f32),
         dma((ctx,)), dma((ctx,)), dma((dp,)), dma((dp,))],
        (up, gp, rate_t, reff_t, eh, feats.T), flops=5 * 10**9)
    output, dmixed, stat = call(
        functools.partial(join_kernel, width),
        [shape((rows, width), bf16), shape((rows, chans), bf16),
         shape((ctx, SUB + modes, chans // ctx))],
        [(modes, wide), (modes, wide), (rows, wide), (rows, wide), (rows, chans), (HALO + rows, chans),
         (count + 1, chans), (modes, wide)],
        (me.reshape(1), qkv, inner_f, inner_b, near, cot, rate_t, reff_t, every, z), scalars=1)

    after = shifted(dmixed[:HALO], "ctx", -1)
    dz, cut = call(
        dz_kernel,
        [shape((rows, chans), bf16), shape((dp, rows, chans // dp), bf16)],
        [(rows + HALO, chans), (rows, chans)],
        (dmixed, after, conv_taps))

    piece = chans // dp
    own_feats = depth // ctx
    unit = (SUB + modes, chans // ctx)
    got, grad_feats, red = exchange(
        tokens_kernel, 2,
        [shape((dp, rows, piece), bf16), shape((rows, depth), bf16), shape(unit)],
        [pltpu.VMEM((depth, chans), bf16), pltpu.VMEM((ctx,) + unit, f32), pltpu.VMEM(unit, f32),
         pltpu.VMEM((dp,) + unit, f32), dma, dma((dp,)), dma((dp,)), dma((ctx,)), dma((ctx,)), dma((dp,)), dma((dp,))],
        (dz, cut, stat, w_in), anywhere=(3,))
    grad_weight, taps = exchange(
        functools.partial(weight_kernel, scale), 3,
        [shape((own_feats, piece), bf16), shape((ctx,) + unit)],
        [pltpu.VMEM((ctx, own_feats, piece), bf16), pltpu.VMEM((ctx, own_feats, piece), bf16),
         pltpu.VMEM((own_feats, piece), f32), dma((ctx,)), dma((ctx,)), dma((ctx,)), dma((ctx,))],
        (toks, got.reshape(dp * rows, piece), red))
    grad_taps = taps[:, :count].transpose(1, 0, 2).reshape(count, chans) * scale
    grad_residues = amp * red[SUB:, :own].T * scale
    return (output[None], grad_feats[None], grad_weight, grad_taps, grad_residues)


def solution(mesh):
    in_specs = (
        P("dp", "ctx", None),
        P(),
        P(),
        P("ctx", None),
        P("ctx", None),
        P("dp", "ctx", None),
    )
    out_specs = (P("dp", "ctx", None), P("dp", "ctx", None), P("ctx", "dp"), P(), P("ctx", None))
    return jax.shard_map(local, mesh=mesh, in_specs=in_specs, out_specs=out_specs, check_vma=False)
```

```python
import functools
import math

import jax
import jax.numpy as jnp
from jax import lax
from jax.experimental import pallas as pl
from jax.experimental.pallas import tpu as pltpu
from jax.sharding import PartitionSpec as P

LANES = 128
SUB = 8
HALO = 16
GROUP = 32

VM = pl.BlockSpec(memory_space=pltpu.VMEM)
SM = pl.BlockSpec(memory_space=pltpu.SMEM)
PARAMS = pltpu.CompilerParams(vmem_limit_bytes=48 << 20)
f32 = jnp.float32
bf16 = jnp.bfloat16


def lane_tiles(width):
    return [(a, min(a + LANES, width)) for a in range(0, width, LANES)]


def sub_index(first, sign, lanes):
    rows = lax.broadcasted_iota(jnp.int32, (SUB, lanes), 0).astype(f32)
    return first + sign * rows


def fold_down(rate, load, blocks, first, sign, order):
    ratio = jnp.exp(-float(SUB) * rate)
    total = None
    for a in order(blocks):
        block = load(a)
        total = block if total is None else total * ratio + block
    weight = jnp.exp(-rate * sub_index(first, sign, rate.shape[1]))
    return jnp.sum(total * weight, axis=0, keepdims=True)


def forwards(blocks):
    return list(range(blocks))


def backwards(blocks):
    return list(range(blocks - 1, -1, -1))


def states_kernel(width, z_ref, taps_ref, cot_ref, rate_ref, qkv_ref, up_ref, gp_ref, eh_ref, zs, mixed):
    rows = cot_ref.shape[0]
    count = taps_ref.shape[0]
    modes, wide = rate_ref.shape
    blocks = rows // SUB
    for a, b in lane_tiles(z_ref.shape[1]):
        zs[:, a:b] = z_ref[:, a:b].astype(f32)
        total = jnp.zeros((rows, b - a), f32)
        for j in range(count):
            total = total + taps_ref[j : j + 1, a:b] * zs[HALO - j : HALO - j + rows, a:b]
        mixed[:, a:b] = total
    if wide > width:
        for part in range(3):
            qkv_ref[part, :, width:] = jnp.zeros((rows, wide - width), f32)
        up_ref[:, width:] = jnp.zeros((2 * rows, wide - width), f32)
        gp_ref[:, width:] = jnp.zeros((2 * rows, wide - width), f32)
    up_ref[:rows, :width] = jnp.zeros((rows, width), f32)
    gp_ref[rows:, :width] = jnp.zeros((rows, width), f32)
    for part in range(3):
        qkv_ref[part, :, :width] = mixed[:, part * width : (part + 1) * width]
    for a, b in lane_tiles(width):
        product = (qkv_ref[1, :, a:b] * qkv_ref[2, :, a:b]).astype(bf16)
        up_ref[rows:, a:b] = product.astype(f32)
        dlong = (cot_ref[:, a:b].astype(f32) * qkv_ref[0, :, a:b]).astype(bf16)
        gp_ref[:rows, a:b] = dlong.astype(f32)
    for a, b in lane_tiles(wide):
        for k in range(modes):
            rate = rate_ref[k : k + 1, a:b]
            eh_ref[k : k + 1, a:b] = fold_down(
                rate, lambda i: up_ref[rows + i * SUB : rows + (i + 1) * SUB, a:b],
                blocks, float(SUB - 1), -1.0, forwards)
            eh_ref[modes + k : modes + k + 1, a:b] = fold_down(
                rate, lambda i: gp_ref[i * SUB : (i + 1) * SUB, a:b], blocks, 0.0, 1.0, backwards)


def spread_modes(rate_ref, coef, ref, lanes, first, sign, order, blocks):
    modes = rate_ref.shape[0]
    totals = [ref[i * SUB : (i + 1) * SUB, lanes] for i in range(blocks)]
    for k in range(modes):
        rate = rate_ref[k : k + 1, lanes]
        ratio = jnp.exp(-float(SUB) * rate)
        term = coef(k) * jnp.exp(-rate * sub_index(first, sign, LANES))
        steps = order(blocks)
        for i in steps:
            totals[i] = totals[i] + term
            if i != steps[-1]:
                term = term * ratio
    for i in range(blocks):
        ref[i * SUB : (i + 1) * SUB, lanes] = totals[i]


def near_kernel(up_ref, gp_ref, rate_ref, reff_ref, inf_ref, inb_ref, near_ref, filt, corr, ups, gps):
    rows = inf_ref.shape[0]
    modes, wide = rate_ref.shape
    blocks = rows // SUB
    inf_ref[...] = jnp.zeros((rows, wide), f32)
    inb_ref[...] = jnp.zeros((rows, wide), f32)
    filt[...] = jnp.zeros((rows, wide), f32)
    index = lax.broadcasted_iota(jnp.int32, (SUB, LANES), 0)

    @pl.loop(0, wide // LANES)
    def _(tile):
        lanes = pl.ds(pl.multiple_of(tile * LANES, LANES), LANES)
        spread_modes(rate_ref, lambda k: reff_ref[k : k + 1, lanes], filt, lanes, 0.0, 1.0, forwards, blocks)
        for s in range(SUB):
            ups[s, SUB:, :] = up_ref[SUB - s : 2 * rows - s, lanes]
            gps[s, : 2 * rows - SUB, :] = gp_ref[s : 2 * rows - SUB + s, lanes]
        for low in range(0, rows, GROUP):
            size = rows - low

            def body(step, carry):
                acc_f, acc_b = carry
                base = pl.multiple_of(low + step * SUB, SUB)
                taps = filt[pl.ds(base, SUB), lanes]
                lags = jnp.zeros((SUB, LANES), f32)
                for s in range(SUB):
                    tap = taps[s : s + 1]
                    moved = ups[s, pl.ds(pl.multiple_of(rows + low - base, SUB), size), :]
                    acc_f = acc_f + tap * moved
                    pair = jnp.sum(gp_ref[low:rows, lanes] * moved, axis=0, keepdims=True)
                    lags = jnp.where(index == s, pair, lags)
                    acc_b = acc_b + tap * gps[s, pl.ds(base, size), :]
                corr[pl.ds(base, SUB), lanes] = lags
                return acc_f, acc_b

            acc_f, acc_b = lax.fori_loop(
                0, GROUP // SUB, body, (inf_ref[low:rows, lanes], inb_ref[0:size, lanes]))
            inf_ref[low:rows, lanes] = acc_f
            inb_ref[0:size, lanes] = acc_b
        for k in range(modes):
            near_ref[k : k + 1, lanes] = fold_down(
                rate_ref[k : k + 1, lanes], lambda i: corr[i * SUB : (i + 1) * SUB, lanes],
                blocks, 0.0, 1.0, backwards)


def join_kernel(width, me_ref, qkv_ref, inf_ref, inb_ref, near_ref, cot_ref, rate_ref, reff_ref, all_ref, z_ref,
                out_ref, dm_ref, stat_ref, first, last, lf, lb, dm, zs, tap_ref, draw_ref):
    rows = cot_ref.shape[0]
    modes, wide = rate_ref.shape
    blocks = rows // SUB
    devices = all_ref.shape[0]
    count = tap_ref.shape[0] - 1
    me = me_ref[0]
    rate = rate_ref[...]
    first[...] = jnp.zeros((modes, wide), f32)
    last[...] = jnp.zeros((modes, wide), f32)

    @pl.loop(0, devices)
    def _(d):
        ahead = jnp.maximum(me - 1 - d, 0).astype(f32)
        keep = jnp.where(d < me, 1.0, 0.0)
        first[...] += keep * jnp.exp(-rate * (ahead * float(rows))) * all_ref[d, 0:modes]
        behind = jnp.maximum(d - me - 1, 0).astype(f32)
        hold = jnp.where(d > me, 1.0, 0.0)
        last[...] += hold * jnp.exp(-rate * (behind * float(rows))) * all_ref[d, modes : 2 * modes]

    draw_ref[...] = near_ref[...] + first[...] * all_ref[me, modes : 2 * modes] * jnp.exp(-rate)
    first[...] = first[...] * reff_ref[...]
    last[...] = last[...] * reff_ref[...]
    lf[...] = inf_ref[...]
    lb[...] = inb_ref[...]

    @pl.loop(0, wide // LANES)
    def _(tile):
        lanes = pl.ds(pl.multiple_of(tile * LANES, LANES), LANES)
        spread_modes(rate_ref, lambda k: first[k : k + 1, lanes], lf, lanes, 1.0, 1.0, forwards, blocks)
        spread_modes(rate_ref, lambda k: last[k : k + 1, lanes], lb, lanes, float(SUB), -1.0, backwards, blocks)

    for a, b in lane_tiles(width):
        far = lf[:, a:b].astype(bf16).astype(f32)
        out_ref[:, a:b] = (qkv_ref[0, :, a:b] * far).astype(bf16)
        lf[:, a:b] = cot_ref[:, a:b].astype(f32) * far
        lb[:, a:b] = lb[:, a:b].astype(bf16).astype(f32)
    dm[:, 0:width] = lf[:, 0:width]
    dm[:, width : 2 * width] = lb[:, 0:width] * qkv_ref[2, :, 0:width]
    dm[:, 2 * width : 3 * width] = lb[:, 0:width] * qkv_ref[1, :, 0:width]
    for a, b in lane_tiles(3 * width):
        held = dm[:, a:b].astype(bf16)
        dm_ref[:, a:b] = held
        held = held.astype(f32)
        zs[:, a:b] = z_ref[:, a:b].astype(f32)
        for j in range(count):
            tap_ref[j : j + 1, a:b] = jnp.sum(
                held * zs[HALO - j : HALO - j + rows, a:b], axis=0, keepdims=True)
    stat_ref[...] = jnp.zeros(stat_ref.shape, f32)
    cols = 3 * width // devices
    own = width // devices
    for d in range(devices):
        stat_ref[d, 0:count, :] = tap_ref[0:count, d * cols : (d + 1) * cols]
        stat_ref[d, SUB : SUB + modes, 0:own] = draw_ref[:, d * own : (d + 1) * own]


def dz_kernel(dm_ref, after_ref, taps_ref, dz_ref, cut_ref, pad, full):
    rows = dm_ref.shape[0]
    parts, _, piece = cut_ref.shape
    count = taps_ref.shape[0]
    for a, b in lane_tiles(dm_ref.shape[1]):
        pad[0:rows, a:b] = dm_ref[:, a:b].astype(f32)
        pad[rows:, a:b] = after_ref[:, a:b].astype(f32)
        total = jnp.zeros((rows, b - a), f32)
        for j in range(count):
            total = total + taps_ref[j : j + 1, a:b] * pad[j : j + rows, a:b]
        dz_ref[:, a:b] = total.astype(bf16)
        full[:, a:b] = total
    for p in range(parts):
        cut_ref[p] = full[:, p * piece : (p + 1) * piece].astype(bf16)


def others(axis):
    size = lax.axis_size(axis)
    me = lax.axis_index(axis)
    return [lax.rem(me + j, size) for j in range(1, size)]


def greet(axes):
    barrier = pltpu.get_barrier_semaphore()
    count = 0
    for axis in axes:
        for peer in others(axis):
            pl.semaphore_signal(barrier, inc=1, device_id={axis: peer}, device_id_type=pl.DeviceIdType.MESH)
            count += 1
    pl.semaphore_wait(barrier, count)


def push(axis, peer, src, dst, send, recv):
    return pltpu.make_async_remote_copy(
        src_ref=src, dst_ref=dst, send_sem=send.at[peer], recv_sem=recv.at[lax.axis_index(axis)],
        device_id={axis: peer}, device_id_type=pl.DeviceIdType.MESH)


def arrival(axis, peer, src, dst, send, recv):
    return pltpu.make_async_remote_copy(
        src_ref=src, dst_ref=dst, send_sem=send.at[peer], recv_sem=recv.at[peer],
        device_id={axis: peer}, device_id_type=pl.DeviceIdType.MESH)


def start_kernel(feats_ref, modal_ref, halo_ref, all_ref, send, recv, hop_send, hop_recv):
    me = lax.axis_index("ctx")
    size = lax.axis_size("ctx")
    rows = feats_ref.shape[0]
    greet(["ctx"])
    hop = pltpu.make_async_remote_copy(
        src_ref=feats_ref.at[pl.ds(rows - HALO, HALO)], dst_ref=halo_ref, send_sem=hop_send, recv_sem=hop_recv,
        device_id={"ctx": lax.rem(me + 1, size)}, device_id_type=pl.DeviceIdType.MESH)
    hop.start()
    sent = [push("ctx", p, modal_ref, all_ref.at[me], send, recv) for p in others("ctx")]
    for copy in sent:
        copy.start()
    all_ref[me] = modal_ref[...]
    hop.wait()

    @pl.when(me == 0)
    def _():
        halo_ref[...] = jnp.zeros(halo_ref.shape, halo_ref.dtype)

    for p in others("ctx"):
        arrival("ctx", p, modal_ref, all_ref.at[p], send, recv).wait_recv()
    for copy in sent:
        copy.wait_send()


def inner_kernel(up_ref, gp_ref, rate_ref, reff_ref, eh_ref, inf_ref, inb_ref, near_ref, all_ref,
                 filt, corr, ups, gps, send, recv):
    me = lax.axis_index("ctx")
    greet(["ctx"])
    sent = [push("ctx", p, eh_ref, all_ref.at[me], send, recv) for p in others("ctx")]
    for copy in sent:
        copy.start()
    all_ref[me] = eh_ref[...]
    near_kernel(up_ref, gp_ref, rate_ref, reff_ref, inf_ref, inb_ref, near_ref, filt, corr, ups, gps)
    for p in others("ctx"):
        arrival("ctx", p, eh_ref, all_ref.at[p], send, recv).wait_recv()
    for copy in sent:
        copy.wait_send()


def tokens_kernel(dm_ref, taps_ref, stat_ref, w_ref, got_ref, feats_ref, red_ref,
                  w_held, after, dz, cut, pad, full, parts, column, rest, w_sem, hop_send, hop_recv,
                  cut_send, cut_recv, st_send, st_recv, col_send, col_recv):
    me = lax.axis_index("ctx")
    size = lax.axis_size("ctx")
    mine = lax.axis_index("dp")
    load = pltpu.make_async_copy(w_ref, w_held, w_sem)
    load.start()
    greet(["ctx", "dp"])
    hop = pltpu.make_async_remote_copy(
        src_ref=dm_ref.at[pl.ds(0, HALO)], dst_ref=after, send_sem=hop_send, recv_sem=hop_recv,
        device_id={"ctx": lax.rem(me + size - 1, size)}, device_id_type=pl.DeviceIdType.MESH)
    hop.start()
    sent = [push("ctx", p, stat_ref.at[p], parts.at[me], st_send, st_recv) for p in others("ctx")]
    for copy in sent:
        copy.start()
    hop.wait()

    @pl.when(me == size - 1)
    def _():
        after[...] = jnp.zeros(after.shape, bf16)

    dz_kernel(dm_ref, after, taps_ref, dz, cut, pad, full)
    swaps = []
    for j, p in enumerate(others("dp")):
        swaps.append(pltpu.make_async_remote_copy(
            src_ref=cut.at[p], dst_ref=got_ref.at[j + 1], send_sem=cut_send.at[j], recv_sem=cut_recv.at[j],
            device_id={"dp": p}, device_id_type=pl.DeviceIdType.MESH))
        swaps[-1].start()
    got_ref[0] = cut[mine]
    total = stat_ref[me]
    for p in others("ctx"):
        arrival("ctx", p, stat_ref.at[p], parts.at[p], st_send, st_recv).wait_recv()
        total = total + parts[p]
    column[...] = total
    spread = [push("dp", p, column, rest.at[mine], col_send, col_recv) for p in others("dp")]
    for copy in spread:
        copy.start()
    load.wait()
    tile = 2 * LANES

    @pl.loop(0, w_held.shape[1] // tile)
    def _(i):
        at = pl.ds(pl.multiple_of(i * tile, tile), tile)
        feats_ref[:, at] = jnp.dot(dz[...], w_held[:, at], preferred_element_type=f32).astype(bf16)

    rest[mine] = column[...]
    for p in others("dp"):
        arrival("dp", p, column, rest.at[p], col_send, col_recv).wait_recv()
    total = rest[0]
    for p in range(1, rest.shape[0]):
        total = total + rest[p]
    red_ref[...] = total
    for copy in swaps:
        copy.wait()
    for copy in sent + spread:
        copy.wait_send()


def weight_kernel(scale, parts, *refs):
    toks = refs[:parts]
    (got_ref, red_ref, gw_ref, taps_ref, term, pairs, land, total,
     pair_send, pair_recv, send, recv, tap_send, tap_recv) = refs[parts:]
    me = lax.axis_index("ctx")
    devices, own, _ = term.shape
    half = devices // 2
    side = lax.rem(me, 2)
    seat = me // 2
    partner = me + 1 - 2 * side
    per = 16 // math.gcd(own, 16)
    count = devices // per
    greet(["ctx"])
    sent = [push("ctx", p, red_ref, taps_ref.at[me], tap_send, tap_recv) for p in others("ctx")]
    for copy in sent:
        copy.start()
    taps_ref[me] = red_ref[...]

    def handover(q, target):
        return pltpu.make_async_remote_copy(
            src_ref=term.at[target], dst_ref=pairs.at[q], send_sem=pair_send.at[q], recv_sem=pair_recv.at[q],
            device_id={"ctx": partner}, device_id_type=pl.DeviceIdType.MESH)

    def delivery(q, slot):
        return pltpu.make_async_remote_copy(
            src_ref=term.at[2 * q + side], dst_ref=land.at[slot], send_sem=send.at[q], recv_sem=recv.at[slot],
            device_id={"ctx": 2 * q + side}, device_id_type=pl.DeviceIdType.MESH)

    @pl.loop(0, count)
    def _(i):
        if per == 1:
            second = i // half
            block = 2 * lax.rem(seat + 1 + lax.rem(i, half), half) + (1 - side) + second * (2 * side - 1)
        else:
            block = i
        at = pl.ds(pl.multiple_of(block * (own * per), 16), own * per)
        rows = jnp.concatenate([tok[at, :] for tok in toks], axis=1)
        piece = jnp.dot(rows, got_ref[...], preferred_element_type=f32)
        for s in range(per):
            target = block * per + s
            term[target] = piece[s * own : (s + 1) * own].astype(bf16)

            @pl.when(lax.rem(target, 2) != side)
            def _():
                handover(target // 2, target).start()

    @pl.loop(1, half)
    def _(j):
        q = lax.rem(seat + j, half)
        target = 2 * q + side
        handover(q, target).wait_recv()
        term[target] = (term[target].astype(f32) + pairs[q].astype(f32)).astype(bf16)
        delivery(q, seat).start()

    handover(seat, me).wait_recv()
    total[...] = term[me].astype(f32) + pairs[seat].astype(f32)

    @pl.loop(1, half)
    def _(j):
        q = lax.rem(seat + j, half)
        delivery(q, q).wait_recv()
        total[...] += land[q].astype(f32)

    gw_ref[...] = (total[...] * scale).astype(bf16)
    for p in others("ctx"):
        arrival("ctx", p, red_ref, taps_ref.at[p], tap_send, tap_recv).wait_recv()
    for copy in sent:
        copy.wait_send()

    @pl.loop(1, half)
    def _(j):
        q = lax.rem(seat + j, half)
        delivery(q, q).wait_send()

    @pl.loop(0, half)
    def _(q):
        handover(q, 2 * q + 1 - side).wait_send()


def shape(dims, kind=f32):
    return jax.ShapeDtypeStruct(dims, kind)


def call(kernel, outs, scratch, ops, scalars=0, flops=10**8):
    return pl.pallas_call(
        kernel,
        out_shape=outs,
        in_specs=[SM] * scalars + [VM] * (len(ops) - scalars),
        out_specs=[VM] * len(outs),
        scratch_shapes=[pltpu.VMEM(dims, f32) for dims in scratch],
        compiler_params=PARAMS,
        cost_estimate=pl.CostEstimate(flops=flops, bytes_accessed=1 << 22, transcendentals=0),
    )(*ops)


def exchange(kernel, number, outs, scratch, ops, anywhere=(), flops=10**8):
    specs = [pl.BlockSpec(memory_space=pl.ANY) if i in anywhere else VM for i in range(len(ops))]
    return pl.pallas_call(
        kernel,
        out_shape=outs,
        in_specs=specs,
        out_specs=[VM] * len(outs),
        scratch_shapes=scratch,
        compiler_params=pltpu.CompilerParams(
            vmem_limit_bytes=48 << 20, collective_id=number, has_side_effects=True),
        cost_estimate=pl.CostEstimate(flops=flops, bytes_accessed=1 << 22, transcendentals=0),
    )(*ops)


def local(tokens, w_in, conv_taps, residues, rates, cotangent):
    feats = tokens[0]
    rows, depth = feats.shape
    cot = cotangent[0]
    width = cot.shape[1]
    chans = w_in.shape[1]
    own, modes = rates.shape
    count = conv_taps.shape[0]
    ctx = lax.axis_size("ctx")
    dp = lax.axis_size("dp")
    me = lax.axis_index("ctx")
    scale = 1.0 / math.sqrt(dp * ctx * rows)
    wide = -(-width // LANES) * LANES

    amp = jnp.sqrt(-jnp.expm1(-2.0 * rates))
    dma = pltpu.SemaphoreType.DMA
    modal = jnp.concatenate([rates.T, (residues * amp).T], axis=0)
    before, modal = exchange(
        start_kernel, 0,
        [shape((HALO, depth), bf16), shape((ctx, 2 * modes, own))],
        [dma((ctx,)), dma((ctx,)), dma, dma],
        (feats, modal))
    modal = modal.transpose(1, 0, 2).reshape(2 * modes, width)
    modal = jnp.pad(modal, ((0, 0), (0, wide - width)))
    rate_t, reff_t = modal[:modes], modal[modes:]

    stacked = jnp.concatenate([before, feats], axis=0)
    z = jnp.dot(stacked, w_in, preferred_element_type=f32).astype(bf16)

    qkv, up, gp, eh = call(
        functools.partial(states_kernel, width),
        [shape((3, rows, wide)), shape((2 * rows, wide)), shape((2 * rows, wide)), shape((2 * modes, wide))],
        [(HALO + rows, chans), (rows, chans)],
        (z, conv_taps, cot, rate_t))
    turned = feats.T
    toks = [turned]
    for j in range(1, dp):
        route = [(i, (i + j) % dp) for i in range(dp)]
        toks.append(lax.ppermute(turned, "dp", route))
    inner_f, inner_b, near, every = exchange(
        inner_kernel, 1,
        [shape((rows, wide)), shape((rows, wide)), shape((modes, wide)), shape((ctx, 2 * modes, wide))],
        [pltpu.VMEM((rows, wide), f32), pltpu.VMEM((rows, wide), f32),
         pltpu.VMEM((SUB, 2 * rows, LANES), f32), pltpu.VMEM((SUB, 2 * rows, LANES), f32),
         dma((ctx,)), dma((ctx,))],
        (up, gp, rate_t, reff_t, eh), flops=5 * 10**9)
    output, dmixed, stat = call(
        functools.partial(join_kernel, width),
        [shape((rows, width), bf16), shape((rows, chans), bf16),
         shape((ctx, SUB + modes, chans // ctx))],
        [(modes, wide), (modes, wide), (rows, wide), (rows, wide), (rows, chans), (HALO + rows, chans),
         (count + 1, chans), (modes, wide)],
        (me.reshape(1), qkv, inner_f, inner_b, near, cot, rate_t, reff_t, every, z), scalars=1)

    piece = chans // dp
    own_feats = depth // ctx
    unit = (SUB + modes, chans // ctx)
    got, grad_feats, red = exchange(
        tokens_kernel, 2,
        [shape((dp, rows, piece), bf16), shape((rows, depth), bf16), shape(unit)],
        [pltpu.VMEM((chans, depth), bf16), pltpu.VMEM((HALO, chans), bf16), pltpu.VMEM((rows, chans), bf16),
         pltpu.VMEM((dp, rows, piece), bf16), pltpu.VMEM((rows + HALO, chans), f32), pltpu.VMEM((rows, chans), f32),
         pltpu.VMEM((ctx,) + unit, f32), pltpu.VMEM(unit, f32), pltpu.VMEM((dp,) + unit, f32),
         dma, dma, dma, dma((dp,)), dma((dp,)), dma((ctx,)), dma((ctx,)), dma((dp,)), dma((dp,))],
        (dmixed, conv_taps, stat, w_in.T), anywhere=(3,))
    half = ctx // 2
    grad_weight, taps = exchange(
        functools.partial(weight_kernel, scale, dp), 3,
        [shape((own_feats, piece), bf16), shape((ctx,) + unit)],
        [pltpu.VMEM((ctx, own_feats, piece), bf16), pltpu.VMEM((half, own_feats, piece), bf16),
         pltpu.VMEM((half, own_feats, piece), bf16), pltpu.VMEM((own_feats, piece), f32),
         dma((half,)), dma((half,)), dma((half,)), dma((half,)), dma((ctx,)), dma((ctx,))],
        (*toks, got.reshape(dp * rows, piece), red))
    grad_taps = taps[:, :count].transpose(1, 0, 2).reshape(count, chans) * scale
    grad_residues = amp * red[SUB:, :own].T * scale
    return (output[None], grad_feats[None], grad_weight, grad_taps, grad_residues)


def solution(mesh):
    in_specs = (
        P("dp", "ctx", None),
        P(),
        P(),
        P("ctx", None),
        P("ctx", None),
        P("dp", "ctx", None),
    )
    out_specs = (P("dp", "ctx", None), P("dp", "ctx", None), P("ctx", "dp"), P(), P("ctx", None))
    return jax.shard_map(local, mesh=mesh, in_specs=in_specs, out_specs=out_specs, check_vma=False)
```

```python
import functools
import math

import jax
import jax.numpy as jnp
from jax import lax
from jax.experimental import pallas as pl
from jax.experimental.pallas import tpu as pltpu
from jax.sharding import PartitionSpec as P

LANES = 128
SUB = 8
HALO = 16
GROUP = 32

VM = pl.BlockSpec(memory_space=pltpu.VMEM)
f32 = jnp.float32
bf16 = jnp.bfloat16


def lane_tiles(width):
    return [(a, min(a + LANES, width)) for a in range(0, width, LANES)]


def sub_index(first, sign, lanes):
    rows = lax.broadcasted_iota(jnp.int32, (SUB, lanes), 0).astype(f32)
    return first + sign * rows


def fold_down(rate, load, blocks, first, sign, order):
    ratio = jnp.exp(-float(SUB) * rate)
    total = None
    for a in order(blocks):
        block = load(a)
        total = block if total is None else total * ratio + block
    weight = jnp.exp(-rate * sub_index(first, sign, rate.shape[1]))
    return jnp.sum(total * weight, axis=0, keepdims=True)


def forwards(blocks):
    return list(range(blocks))


def backwards(blocks):
    return list(range(blocks - 1, -1, -1))


def states_kernel(width, z_ref, taps_ref, cot_ref, rate_ref, qkv_ref, up_ref, gp_ref, eh_ref, zs, mixed):
    rows = cot_ref.shape[0]
    count = taps_ref.shape[0]
    modes, wide = rate_ref.shape
    blocks = rows // SUB
    for a, b in lane_tiles(z_ref.shape[1]):
        zs[:, a:b] = z_ref[:, a:b].astype(f32)
        total = jnp.zeros((rows, b - a), f32)
        for j in range(count):
            total = total + taps_ref[j : j + 1, a:b] * zs[HALO - j : HALO - j + rows, a:b]
        mixed[:, a:b] = total
    if wide > width:
        for part in range(3):
            qkv_ref[part, :, width:] = jnp.zeros((rows, wide - width), f32)
        up_ref[:, width:] = jnp.zeros((2 * rows, wide - width), f32)
        gp_ref[:, width:] = jnp.zeros((2 * rows, wide - width), f32)
    up_ref[:rows, :width] = jnp.zeros((rows, width), f32)
    gp_ref[rows:, :width] = jnp.zeros((rows, width), f32)
    for part in range(3):
        qkv_ref[part, :, :width] = mixed[:, part * width : (part + 1) * width]
    for a, b in lane_tiles(width):
        product = (qkv_ref[1, :, a:b] * qkv_ref[2, :, a:b]).astype(bf16)
        up_ref[rows:, a:b] = product.astype(f32)
        dlong = (cot_ref[:, a:b].astype(f32) * qkv_ref[0, :, a:b]).astype(bf16)
        gp_ref[:rows, a:b] = dlong.astype(f32)
    for a, b in lane_tiles(wide):
        for k in range(modes):
            rate = rate_ref[k : k + 1, a:b]
            eh_ref[k : k + 1, a:b] = fold_down(
                rate, lambda i: up_ref[rows + i * SUB : rows + (i + 1) * SUB, a:b],
                blocks, float(SUB - 1), -1.0, forwards)
            eh_ref[modes + k : modes + k + 1, a:b] = fold_down(
                rate, lambda i: gp_ref[i * SUB : (i + 1) * SUB, a:b], blocks, 0.0, 1.0, backwards)


def spread_modes(rate_ref, coef, ref, lanes, first, sign, order, blocks):
    modes = rate_ref.shape[0]
    totals = [ref[i * SUB : (i + 1) * SUB, lanes] for i in range(blocks)]
    for k in range(modes):
        rate = rate_ref[k : k + 1, lanes]
        ratio = jnp.exp(-float(SUB) * rate)
        term = coef(k) * jnp.exp(-rate * sub_index(first, sign, LANES))
        steps = order(blocks)
        for i in steps:
            totals[i] = totals[i] + term
            if i != steps[-1]:
                term = term * ratio
    for i in range(blocks):
        ref[i * SUB : (i + 1) * SUB, lanes] = totals[i]


def near_kernel(up_ref, gp_ref, rate_ref, reff_ref, inf_ref, inb_ref, near_ref, filt, corr, ups, gps):
    rows = inf_ref.shape[0]
    modes, wide = rate_ref.shape
    blocks = rows // SUB
    inf_ref[...] = jnp.zeros((rows, wide), f32)
    inb_ref[...] = jnp.zeros((rows, wide), f32)
    filt[...] = jnp.zeros((rows, wide), f32)
    index = lax.broadcasted_iota(jnp.int32, (SUB, LANES), 0)

    @pl.loop(0, wide // LANES)
    def _(tile):
        lanes = pl.ds(pl.multiple_of(tile * LANES, LANES), LANES)
        spread_modes(rate_ref, lambda k: reff_ref[k : k + 1, lanes], filt, lanes, 0.0, 1.0, forwards, blocks)
        for s in range(SUB):
            ups[s, SUB:, :] = up_ref[SUB - s : 2 * rows - s, lanes]
            gps[s, : 2 * rows - SUB, :] = gp_ref[s : 2 * rows - SUB + s, lanes]
        for low in range(0, rows, GROUP):
            size = rows - low

            def body(step, carry):
                acc_f, acc_b = carry
                base = pl.multiple_of(low + step * SUB, SUB)
                taps = filt[pl.ds(base, SUB), lanes]
                lags = jnp.zeros((SUB, LANES), f32)
                for s in range(SUB):
                    tap = taps[s : s + 1]
                    moved = ups[s, pl.ds(pl.multiple_of(rows + low - base, SUB), size), :]
                    acc_f = acc_f + tap * moved
                    pair = jnp.sum(gp_ref[low:rows, lanes] * moved, axis=0, keepdims=True)
                    lags = jnp.where(index == s, pair, lags)
                    acc_b = acc_b + tap * gps[s, pl.ds(base, size), :]
                corr[pl.ds(base, SUB), lanes] = lags
                return acc_f, acc_b

            acc_f, acc_b = lax.fori_loop(
                0, GROUP // SUB, body, (inf_ref[low:rows, lanes], inb_ref[0:size, lanes]))
            inf_ref[low:rows, lanes] = acc_f
            inb_ref[0:size, lanes] = acc_b
        for k in range(modes):
            near_ref[k : k + 1, lanes] = fold_down(
                rate_ref[k : k + 1, lanes], lambda i: corr[i * SUB : (i + 1) * SUB, lanes],
                blocks, 0.0, 1.0, backwards)


def join_kernel(width, me, qkv_ref, lf, lb, near_ref, cot_ref, rate_ref, reff_ref, all_ref, zs,
                out_ref, dm_ref, stat_ref, first, last, dm, tap_ref, draw_ref):
    rows = cot_ref.shape[0]
    modes, wide = rate_ref.shape
    blocks = rows // SUB
    devices = all_ref.shape[0]
    count = tap_ref.shape[0] - 1
    rate = rate_ref[...]
    first[...] = jnp.zeros((modes, wide), f32)
    last[...] = jnp.zeros((modes, wide), f32)

    @pl.loop(0, devices)
    def _(d):
        ahead = jnp.maximum(me - 1 - d, 0).astype(f32)
        keep = jnp.where(d < me, 1.0, 0.0)
        first[...] += keep * jnp.exp(-rate * (ahead * float(rows))) * all_ref[d, 0:modes]
        behind = jnp.maximum(d - me - 1, 0).astype(f32)
        hold = jnp.where(d > me, 1.0, 0.0)
        last[...] += hold * jnp.exp(-rate * (behind * float(rows))) * all_ref[d, modes : 2 * modes]

    draw_ref[...] = near_ref[...] + first[...] * all_ref[me, modes : 2 * modes] * jnp.exp(-rate)
    first[...] = first[...] * reff_ref[...]
    last[...] = last[...] * reff_ref[...]

    @pl.loop(0, wide // LANES)
    def _(tile):
        lanes = pl.ds(pl.multiple_of(tile * LANES, LANES), LANES)
        spread_modes(rate_ref, lambda k: first[k : k + 1, lanes], lf, lanes, 1.0, 1.0, forwards, blocks)
        spread_modes(rate_ref, lambda k: last[k : k + 1, lanes], lb, lanes, float(SUB), -1.0, backwards, blocks)

    for a, b in lane_tiles(width):
        far = lf[:, a:b].astype(bf16).astype(f32)
        out_ref[:, a:b] = (qkv_ref[0, :, a:b] * far).astype(bf16)
        lf[:, a:b] = cot_ref[:, a:b].astype(f32) * far
        lb[:, a:b] = lb[:, a:b].astype(bf16).astype(f32)
    dm[:, 0:width] = lf[:, 0:width]
    dm[:, width : 2 * width] = lb[:, 0:width] * qkv_ref[2, :, 0:width]
    dm[:, 2 * width : 3 * width] = lb[:, 0:width] * qkv_ref[1, :, 0:width]
    for a, b in lane_tiles(3 * width):
        held = dm[:, a:b].astype(bf16)
        dm_ref[:, a:b] = held
        held = held.astype(f32)
        for j in range(count):
            tap_ref[j : j + 1, a:b] = jnp.sum(
                held * zs[HALO - j : HALO - j + rows, a:b], axis=0, keepdims=True)
    stat_ref[...] = jnp.zeros(stat_ref.shape, f32)
    cols = 3 * width // devices
    own = width // devices
    for d in range(devices):
        stat_ref[d, 0:count, :] = tap_ref[0:count, d * cols : (d + 1) * cols]
        stat_ref[d, SUB : SUB + modes, 0:own] = draw_ref[:, d * own : (d + 1) * own]


def dz_kernel(dm_ref, after_ref, taps_ref, dz_ref, cut_ref, pad, full):
    rows = dm_ref.shape[0]
    parts, _, piece = cut_ref.shape
    count = taps_ref.shape[0]
    for a, b in lane_tiles(dm_ref.shape[1]):
        pad[0:rows, a:b] = dm_ref[:, a:b].astype(f32)
        pad[rows:, a:b] = after_ref[:, a:b].astype(f32)
        total = jnp.zeros((rows, b - a), f32)
        for j in range(count):
            total = total + taps_ref[j : j + 1, a:b] * pad[j : j + rows, a:b]
        dz_ref[:, a:b] = total.astype(bf16)
        full[:, a:b] = total
    for p in range(parts):
        cut_ref[p] = full[:, p * piece : (p + 1) * piece].astype(bf16)


def others(axis):
    size = lax.axis_size(axis)
    me = lax.axis_index(axis)
    return [lax.rem(me + j, size) for j in range(1, size)]


def greet(axes):
    barrier = pltpu.get_barrier_semaphore()
    count = 0
    for axis in axes:
        for peer in others(axis):
            pl.semaphore_signal(barrier, inc=1, device_id={axis: peer}, device_id_type=pl.DeviceIdType.MESH)
            count += 1
    pl.semaphore_wait(barrier, count)


def push(axis, peer, src, dst, send, recv):
    return pltpu.make_async_remote_copy(
        src_ref=src, dst_ref=dst, send_sem=send.at[peer], recv_sem=recv.at[lax.axis_index(axis)],
        device_id={axis: peer}, device_id_type=pl.DeviceIdType.MESH)


def arrival(axis, peer, src, dst, send, recv):
    return pltpu.make_async_remote_copy(
        src_ref=src, dst_ref=dst, send_sem=send.at[peer], recv_sem=recv.at[peer],
        device_id={axis: peer}, device_id_type=pl.DeviceIdType.MESH)


def tokens_part(dm_ref, taps_ref, stat_ref, w_held, got_ref, feats_ref, red_ref,
                  after, dz, cut, pad, full, parts, column, rest, hop_send, hop_recv,
                  cut_send, cut_recv, st_send, st_recv, col_send, col_recv):
    me = lax.axis_index("ctx")
    size = lax.axis_size("ctx")
    mine = lax.axis_index("dp")
    hop = pltpu.make_async_remote_copy(
        src_ref=dm_ref.at[pl.ds(0, HALO)], dst_ref=after, send_sem=hop_send, recv_sem=hop_recv,
        device_id={"ctx": lax.rem(me + size - 1, size)}, device_id_type=pl.DeviceIdType.MESH)
    hop.start()
    sent = [push("ctx", p, stat_ref.at[p], parts.at[me], st_send, st_recv) for p in others("ctx")]
    for copy in sent:
        copy.start()
    hop.wait()

    @pl.when(me == size - 1)
    def _():
        after[...] = jnp.zeros(after.shape, bf16)

    dz_kernel(dm_ref, after, taps_ref, dz, cut, pad, full)
    swaps = []
    for j, p in enumerate(others("dp")):
        swaps.append(pltpu.make_async_remote_copy(
            src_ref=cut.at[p], dst_ref=got_ref.at[j + 1], send_sem=cut_send.at[j], recv_sem=cut_recv.at[j],
            device_id={"dp": p}, device_id_type=pl.DeviceIdType.MESH))
        swaps[-1].start()
    got_ref[0] = cut[mine]
    total = stat_ref[me]
    for p in others("ctx"):
        arrival("ctx", p, stat_ref.at[p], parts.at[p], st_send, st_recv).wait_recv()
        total = total + parts[p]
    column[...] = total
    spread = [push("dp", p, column, rest.at[mine], col_send, col_recv) for p in others("dp")]
    for copy in spread:
        copy.start()
    tile = 2 * LANES

    @pl.loop(0, w_held.shape[1] // tile)
    def _(i):
        at = pl.ds(pl.multiple_of(i * tile, tile), tile)
        feats_ref[:, at] = jnp.dot(dz[...], w_held[:, at], preferred_element_type=f32).astype(bf16)

    rest[mine] = column[...]
    for p in others("dp"):
        arrival("dp", p, column, rest.at[p], col_send, col_recv).wait_recv()
    total = rest[0]
    for p in range(1, rest.shape[0]):
        total = total + rest[p]
    red_ref[...] = total
    for copy in swaps:
        copy.wait()
    for copy in sent + spread:
        copy.wait_send()


def weight_part(scale, toks, got_ref, red_ref, gw_ref, taps_ref, term, pairs, land, total,
                pair_send, pair_recv, send, recv, tap_send, tap_recv):
    me = lax.axis_index("ctx")
    devices, own, _ = term.shape
    half = devices // 2
    side = lax.rem(me, 2)
    seat = me // 2
    partner = me + 1 - 2 * side
    per = 16 // math.gcd(own, 16)
    count = devices // per
    depth = got_ref.shape[0] * got_ref.shape[1]
    sent = [push("ctx", p, red_ref, taps_ref.at[me], tap_send, tap_recv) for p in others("ctx")]
    for copy in sent:
        copy.start()
    taps_ref[me] = red_ref[...]

    def handover(q, target):
        return pltpu.make_async_remote_copy(
            src_ref=term.at[target], dst_ref=pairs.at[q], send_sem=pair_send.at[q], recv_sem=pair_recv.at[q],
            device_id={"ctx": partner}, device_id_type=pl.DeviceIdType.MESH)

    def delivery(q, slot):
        return pltpu.make_async_remote_copy(
            src_ref=term.at[2 * q + side], dst_ref=land.at[slot], send_sem=send.at[q], recv_sem=recv.at[slot],
            device_id={"ctx": 2 * q + side}, device_id_type=pl.DeviceIdType.MESH)

    @pl.loop(0, count)
    def _(i):
        if per == 1:
            second = i // half
            block = 2 * lax.rem(seat + 1 + lax.rem(i, half), half) + (1 - side) + second * (2 * side - 1)
        else:
            block = i
        at = pl.ds(pl.multiple_of(block * (own * per), 16), own * per)
        rows = jnp.concatenate([toks[j, at, :] for j in range(toks.shape[0])], axis=1)
        piece = jnp.dot(rows, got_ref[...].reshape(depth, -1), preferred_element_type=f32)
        for s in range(per):
            target = block * per + s
            term[target] = piece[s * own : (s + 1) * own].astype(bf16)

            @pl.when(lax.rem(target, 2) != side)
            def _():
                handover(target // 2, target).start()

    @pl.loop(1, half)
    def _(j):
        q = lax.rem(seat + j, half)
        target = 2 * q + side
        handover(q, target).wait_recv()
        term[target] = (term[target].astype(f32) + pairs[q].astype(f32)).astype(bf16)
        delivery(q, seat).start()

    handover(seat, me).wait_recv()
    total[...] = term[me].astype(f32) + pairs[seat].astype(f32)

    @pl.loop(1, half)
    def _(j):
        q = lax.rem(seat + j, half)
        delivery(q, q).wait_recv()
        total[...] += land[q].astype(f32)

    gw_ref[...] = (total[...] * scale).astype(bf16)
    for p in others("ctx"):
        arrival("ctx", p, red_ref, taps_ref.at[p], tap_send, tap_recv).wait_recv()
    for copy in sent:
        copy.wait_send()

    @pl.loop(1, half)
    def _(j):
        q = lax.rem(seat + j, half)
        delivery(q, q).wait_send()

    @pl.loop(0, half)
    def _(q):
        handover(q, 2 * q + 1 - side).wait_send()


def shape(dims, kind=f32):
    return jax.ShapeDtypeStruct(dims, kind)


def operator_kernel(width, scale, feats_ref, taps_ref, cot_ref, modal_ref, w_ref,
                    out_ref, gf_ref, gw_ref, gt_ref, red_ref,
                    w_held, stack, toks, modal_all, rate, reff, z, zs, mixed, qkv, up, gp, eh, every,
                    inf, inb, near, filt, corr, ups, gps, first, last, dm, dm16, tap, draw, stat,
                    after, dz, cut, full, parts, column, rest, got, term, pairs, land, total, taps_all,
                    w_sem, hop_send, hop_recv, tok_send, tok_recv, mod_send, mod_recv, st_send, st_recv,
                    aft_send, aft_recv, cut_send, cut_recv, part_send, part_recv, col_send, col_recv,
                    pair_send, pair_recv, land_send, land_recv, tap_send, tap_recv):
    me = lax.axis_index("ctx")
    size = lax.axis_size("ctx")
    rows, depth = feats_ref.shape
    chans = w_held.shape[0]
    modes, wide = rate.shape
    own = width // size
    count = taps_ref.shape[0]
    cuts = [(a, min(a + 6 * LANES, chans)) for a in range(0, chans, 6 * LANES)]
    loads = [pltpu.make_async_copy(w_ref.at[a:b], w_held.at[a:b], w_sem.at[i]) for i, (a, b) in enumerate(cuts)]
    for copy in loads:
        copy.start()
    greet(["ctx", "dp"])
    hop = pltpu.make_async_remote_copy(
        src_ref=feats_ref.at[pl.ds(rows - HALO, HALO)], dst_ref=stack.at[pl.ds(0, HALO)],
        send_sem=hop_send, recv_sem=hop_recv,
        device_id={"ctx": lax.rem(me + 1, size)}, device_id_type=pl.DeviceIdType.MESH)
    hop.start()
    sent = [push("ctx", p, modal_ref, modal_all.at[me], mod_send, mod_recv) for p in others("ctx")]
    for copy in sent:
        copy.start()
    for a, b in lane_tiles(depth):
        toks[0, a:b, :] = feats_ref[:, a:b].astype(f32).T.astype(bf16)
    swaps = []
    for j, p in enumerate(others("dp")):
        swaps.append(pltpu.make_async_remote_copy(
            src_ref=toks.at[0], dst_ref=toks.at[j + 1], send_sem=tok_send.at[j], recv_sem=tok_recv.at[j],
            device_id={"dp": p}, device_id_type=pl.DeviceIdType.MESH))
        swaps[-1].start()
    stack[HALO:, :] = feats_ref[...]
    hop.wait()

    @pl.when(me == 0)
    def _():
        stack[0:HALO, :] = jnp.zeros((HALO, depth), bf16)

    for i, (a, b) in enumerate(cuts):
        loads[i].wait()
        z[:, a:b] = lax.dot_general(
            stack[...], w_held[a:b, :], (((1,), (1,)), ((), ())), preferred_element_type=f32).astype(bf16)
    modal_all[me] = modal_ref[...]
    for p in others("ctx"):
        arrival("ctx", p, modal_ref, modal_all.at[p], mod_send, mod_recv).wait_recv()
    rate[...] = jnp.zeros((modes, wide), f32)
    reff[...] = jnp.zeros((modes, wide), f32)
    for d in range(size):
        rate[:, d * own : (d + 1) * own] = modal_all[d, 0:modes]
        reff[:, d * own : (d + 1) * own] = modal_all[d, modes : 2 * modes]

    states_kernel(width, z, taps_ref, cot_ref, rate, qkv, up, gp, eh, zs, mixed)
    flow = [push("ctx", p, eh, every.at[me], st_send, st_recv) for p in others("ctx")]
    for copy in flow:
        copy.start()
    every[me] = eh[...]
    near_kernel(up, gp, rate, reff, inf, inb, near, filt, corr, ups, gps)
    for p in others("ctx"):
        arrival("ctx", p, eh, every.at[p], st_send, st_recv).wait_recv()
    join_kernel(width, me, qkv, inf, inb, near, cot_ref, rate, reff, every, zs,
                out_ref, dm16, stat, first, last, dm, tap, draw)
    tokens_part(dm16, taps_ref, stat, w_held, got, gf_ref, red_ref,
                after, dz, cut, zs, full, parts, column, rest, aft_send, aft_recv,
                cut_send, cut_recv, part_send, part_recv, col_send, col_recv)
    for copy in swaps:
        copy.wait()
    weight_part(scale, toks, got, red_ref, gw_ref, taps_all, term, pairs, land, total,
                pair_send, pair_recv, land_send, land_recv, tap_send, tap_recv)
    unit = chans // size
    for d in range(size):
        gt_ref[:, d * unit : (d + 1) * unit] = taps_all[d, 0:count, :] * scale
    for copy in sent + flow:
        copy.wait_send()


def local(tokens, w_in, conv_taps, residues, rates, cotangent):
    feats = tokens[0]
    rows, depth = feats.shape
    cot = cotangent[0]
    width = cot.shape[1]
    chans = w_in.shape[1]
    own, modes = rates.shape
    count = conv_taps.shape[0]
    ctx = lax.axis_size("ctx")
    dp = lax.axis_size("dp")
    me = lax.axis_index("ctx")
    scale = 1.0 / math.sqrt(dp * ctx * rows)
    wide = -(-width // LANES) * LANES

    amp = jnp.sqrt(-jnp.expm1(-2.0 * rates))
    modal = jnp.concatenate([rates.T, (residues * amp).T], axis=0)
    dma = pltpu.SemaphoreType.DMA
    piece = chans // dp
    own_feats = depth // ctx
    half = ctx // 2
    unit = (SUB + modes, chans // ctx)

    def held(*dims):
        return pltpu.VMEM(dims, f32)

    def short(*dims):
        return pltpu.VMEM(dims, bf16)

    scratch = [
        short(chans, depth), short(HALO + rows, depth), short(dp, depth, rows),
        held(ctx, 2 * modes, own), held(modes, wide), held(modes, wide), short(HALO + rows, chans),
        held(HALO + rows, chans), held(rows, chans), held(3, rows, wide), held(2 * rows, wide),
        held(2 * rows, wide), held(2 * modes, wide), held(ctx, 2 * modes, wide),
        held(rows, wide), held(rows, wide), held(modes, wide), held(rows, wide), held(rows, wide),
        held(SUB, 2 * rows, LANES), held(SUB, 2 * rows, LANES), held(modes, wide), held(modes, wide),
        held(rows, chans), short(rows, chans), held(count + 1, chans), held(modes, wide), held(ctx, *unit),
        short(HALO, chans), short(rows, chans), short(dp, rows, piece), held(rows, chans),
        held(ctx, *unit), held(*unit), held(dp, *unit), short(dp, rows, piece),
        short(ctx, own_feats, piece), short(half, own_feats, piece), short(half, own_feats, piece),
        held(own_feats, piece), held(ctx, *unit),
        dma((-(-chans // (6 * LANES)),)), dma, dma, dma((dp,)), dma((dp,)), dma((ctx,)), dma((ctx,)),
        dma((ctx,)), dma((ctx,)), dma, dma, dma((dp,)), dma((dp,)), dma((ctx,)), dma((ctx,)),
        dma((dp,)), dma((dp,)), dma((half,)), dma((half,)), dma((half,)), dma((half,)), dma((ctx,)), dma((ctx,)),
    ]
    output, grad_feats, grad_weight, grad_taps, red = pl.pallas_call(
        functools.partial(operator_kernel, width, scale),
        out_shape=[shape((rows, width), bf16), shape((rows, depth), bf16), shape((own_feats, piece), bf16),
                   shape((count, chans)), shape(unit)],
        in_specs=[VM] * 4 + [pl.BlockSpec(memory_space=pl.ANY)],
        out_specs=[VM] * 5,
        scratch_shapes=scratch,
        compiler_params=pltpu.CompilerParams(
            vmem_limit_bytes=56 << 20, collective_id=0, has_side_effects=True),
        cost_estimate=pl.CostEstimate(flops=10**10, bytes_accessed=1 << 24, transcendentals=0),
    )(feats, conv_taps, cot, modal, w_in.T)
    grad_residues = amp * red[SUB:, :own].T * scale
    return (output[None], grad_feats[None], grad_weight, grad_taps, grad_residues)


def solution(mesh):
    in_specs = (
        P("dp", "ctx", None),
        P(),
        P(),
        P("ctx", None),
        P("ctx", None),
        P("dp", "ctx", None),
    )
    out_specs = (P("dp", "ctx", None), P("dp", "ctx", None), P("ctx", "dp"), P(), P("ctx", None))
    return jax.shard_map(local, mesh=mesh, in_specs=in_specs, out_specs=out_specs, check_vma=False)
```

```python
import functools
import math

import jax
import jax.numpy as jnp
from jax import lax
from jax.experimental import pallas as pl
from jax.experimental.pallas import tpu as pltpu
from jax.sharding import PartitionSpec as P

LANES = 128
SUB = 8
HALO = 16
GROUP = 16

VM = pl.BlockSpec(memory_space=pltpu.VMEM)
f32 = jnp.float32
bf16 = jnp.bfloat16


def lane_tiles(width):
    return [(a, min(a + LANES, width)) for a in range(0, width, LANES)]


def sub_index(first, sign, lanes):
    rows = lax.broadcasted_iota(jnp.int32, (SUB, lanes), 0).astype(f32)
    return first + sign * rows


def fold_down(rate, load, blocks, first, sign, order):
    ratio = jnp.exp(-float(SUB) * rate)
    total = None
    for a in order(blocks):
        block = load(a)
        total = block if total is None else total * ratio + block
    weight = jnp.exp(-rate * sub_index(first, sign, rate.shape[1]))
    return jnp.sum(total * weight, axis=0, keepdims=True)


def forwards(blocks):
    return list(range(blocks))


def backwards(blocks):
    return list(range(blocks - 1, -1, -1))


def states_kernel(width, z_ref, taps_ref, cot_ref, rate_ref, qkv_ref, up_ref, gp_ref, eh_ref, zs, mixed):
    rows = cot_ref.shape[0]
    count = taps_ref.shape[0]
    modes, wide = rate_ref.shape
    blocks = rows // SUB
    for a, b in lane_tiles(z_ref.shape[1]):
        zs[:, a:b] = z_ref[:, a:b].astype(f32)
        total = jnp.zeros((rows, b - a), f32)
        for j in range(count):
            total = total + taps_ref[j : j + 1, a:b] * zs[HALO - j : HALO - j + rows, a:b]
        mixed[:, a:b] = total
    if wide > width:
        for part in range(3):
            qkv_ref[part, :, width:] = jnp.zeros((rows, wide - width), f32)
        up_ref[:, width:] = jnp.zeros((2 * rows, wide - width), f32)
        gp_ref[:, width:] = jnp.zeros((2 * rows, wide - width), f32)
    up_ref[:rows, :width] = jnp.zeros((rows, width), f32)
    gp_ref[rows:, :width] = jnp.zeros((rows, width), f32)
    for part in range(3):
        qkv_ref[part, :, :width] = mixed[:, part * width : (part + 1) * width]
    for a, b in lane_tiles(width):
        product = (qkv_ref[1, :, a:b] * qkv_ref[2, :, a:b]).astype(bf16)
        up_ref[rows:, a:b] = product.astype(f32)
        dlong = (cot_ref[:, a:b].astype(f32) * qkv_ref[0, :, a:b]).astype(bf16)
        gp_ref[:rows, a:b] = dlong.astype(f32)
    for a, b in lane_tiles(wide):
        for k in range(modes):
            rate = rate_ref[k : k + 1, a:b]
            eh_ref[k : k + 1, a:b] = fold_down(
                rate, lambda i: up_ref[rows + i * SUB : rows + (i + 1) * SUB, a:b],
                blocks, float(SUB - 1), -1.0, forwards)
            eh_ref[modes + k : modes + k + 1, a:b] = fold_down(
                rate, lambda i: gp_ref[i * SUB : (i + 1) * SUB, a:b], blocks, 0.0, 1.0, backwards)


def spread_modes(rate_ref, coef, ref, lanes, first, sign, order, blocks):
    modes = rate_ref.shape[0]
    totals = [ref[i * SUB : (i + 1) * SUB, lanes] for i in range(blocks)]
    for k in range(modes):
        rate = rate_ref[k : k + 1, lanes]
        ratio = jnp.exp(-float(SUB) * rate)
        term = coef(k) * jnp.exp(-rate * sub_index(first, sign, LANES))
        steps = order(blocks)
        for i in steps:
            totals[i] = totals[i] + term
            if i != steps[-1]:
                term = term * ratio
    for i in range(blocks):
        ref[i * SUB : (i + 1) * SUB, lanes] = totals[i]


def near_kernel(up_ref, gp_ref, rate_ref, reff_ref, inf_ref, inb_ref, near_ref, filt, corr, ups, gps):
    rows = inf_ref.shape[0]
    modes, wide = rate_ref.shape
    blocks = rows // SUB
    inf_ref[...] = jnp.zeros((rows, wide), f32)
    inb_ref[...] = jnp.zeros((rows, wide), f32)
    filt[...] = jnp.zeros((rows, wide), f32)
    index = lax.broadcasted_iota(jnp.int32, (SUB, LANES), 0)

    @pl.loop(0, wide // LANES)
    def _(tile):
        lanes = pl.ds(pl.multiple_of(tile * LANES, LANES), LANES)
        spread_modes(rate_ref, lambda k: reff_ref[k : k + 1, lanes], filt, lanes, 0.0, 1.0, forwards, blocks)
        for s in range(SUB):
            ups[s, SUB:, :] = up_ref[SUB - s : 2 * rows - s, lanes]
            gps[s, : 2 * rows - SUB, :] = gp_ref[s : 2 * rows - SUB + s, lanes]
        for low in range(0, rows, GROUP):
            size = rows - low

            def body(step, carry):
                acc_f, acc_b = carry
                base = pl.multiple_of(low + step * SUB, SUB)
                taps = filt[pl.ds(base, SUB), lanes]
                lags = jnp.zeros((SUB, LANES), f32)
                for s in range(SUB):
                    tap = taps[s : s + 1]
                    moved = ups[s, pl.ds(pl.multiple_of(rows + low - base, SUB), size), :]
                    acc_f = acc_f + tap * moved
                    pair = jnp.sum(gp_ref[low:rows, lanes] * moved, axis=0, keepdims=True)
                    lags = jnp.where(index == s, pair, lags)
                    acc_b = acc_b + tap * gps[s, pl.ds(base, size), :]
                corr[pl.ds(base, SUB), lanes] = lags
                return acc_f, acc_b

            acc_f, acc_b = lax.fori_loop(
                0, GROUP // SUB, body, (inf_ref[low:rows, lanes], inb_ref[0:size, lanes]))
            inf_ref[low:rows, lanes] = acc_f
            inb_ref[0:size, lanes] = acc_b
        for k in range(modes):
            near_ref[k : k + 1, lanes] = fold_down(
                rate_ref[k : k + 1, lanes], lambda i: corr[i * SUB : (i + 1) * SUB, lanes],
                blocks, 0.0, 1.0, backwards)


def join_kernel(width, me, qkv_ref, lf, lb, near_ref, cot_ref, rate_ref, reff_ref, all_ref, zs,
                out_ref, dm_ref, stat_ref, first, last, dm, tap_ref, draw_ref):
    rows = cot_ref.shape[0]
    modes, wide = rate_ref.shape
    blocks = rows // SUB
    devices = all_ref.shape[0]
    count = tap_ref.shape[0] - 1
    rate = rate_ref[...]
    first[...] = jnp.zeros((modes, wide), f32)
    last[...] = jnp.zeros((modes, wide), f32)

    @pl.loop(0, devices)
    def _(d):
        ahead = jnp.maximum(me - 1 - d, 0).astype(f32)
        keep = jnp.where(d < me, 1.0, 0.0)
        first[...] += keep * jnp.exp(-rate * (ahead * float(rows))) * all_ref[d, 0:modes]
        behind = jnp.maximum(d - me - 1, 0).astype(f32)
        hold = jnp.where(d > me, 1.0, 0.0)
        last[...] += hold * jnp.exp(-rate * (behind * float(rows))) * all_ref[d, modes : 2 * modes]

    draw_ref[...] = near_ref[...] + first[...] * all_ref[me, modes : 2 * modes] * jnp.exp(-rate)
    first[...] = first[...] * reff_ref[...]
    last[...] = last[...] * reff_ref[...]

    @pl.loop(0, wide // LANES)
    def _(tile):
        lanes = pl.ds(pl.multiple_of(tile * LANES, LANES), LANES)
        spread_modes(rate_ref, lambda k: first[k : k + 1, lanes], lf, lanes, 1.0, 1.0, forwards, blocks)
        spread_modes(rate_ref, lambda k: last[k : k + 1, lanes], lb, lanes, float(SUB), -1.0, backwards, blocks)

    for a, b in lane_tiles(width):
        far = lf[:, a:b].astype(bf16).astype(f32)
        out_ref[:, a:b] = (qkv_ref[0, :, a:b] * far).astype(bf16)
        lf[:, a:b] = cot_ref[:, a:b].astype(f32) * far
        lb[:, a:b] = lb[:, a:b].astype(bf16).astype(f32)
    dm[:, 0:width] = lf[:, 0:width]
    dm[:, width : 2 * width] = lb[:, 0:width] * qkv_ref[2, :, 0:width]
    dm[:, 2 * width : 3 * width] = lb[:, 0:width] * qkv_ref[1, :, 0:width]
    for a, b in lane_tiles(3 * width):
        held = dm[:, a:b].astype(bf16)
        dm_ref[:, a:b] = held
        held = held.astype(f32)
        for j in range(count):
            tap_ref[j : j + 1, a:b] = jnp.sum(
                held * zs[HALO - j : HALO - j + rows, a:b], axis=0, keepdims=True)
    stat_ref[...] = jnp.zeros(stat_ref.shape, f32)
    cols = 3 * width // devices
    own = width // devices
    for d in range(devices):
        stat_ref[d, 0:count, :] = tap_ref[0:count, d * cols : (d + 1) * cols]
        stat_ref[d, SUB : SUB + modes, 0:own] = draw_ref[:, d * own : (d + 1) * own]


def dz_kernel(dm_ref, after_ref, taps_ref, dz_ref, cut_ref, pad, full):
    rows = dm_ref.shape[0]
    parts, _, piece = cut_ref.shape
    count = taps_ref.shape[0]
    for a, b in lane_tiles(dm_ref.shape[1]):
        pad[0:rows, a:b] = dm_ref[:, a:b].astype(f32)
        pad[rows:, a:b] = after_ref[:, a:b].astype(f32)
        total = jnp.zeros((rows, b - a), f32)
        for j in range(count):
            total = total + taps_ref[j : j + 1, a:b] * pad[j : j + rows, a:b]
        dz_ref[:, a:b] = total.astype(bf16)
        full[:, a:b] = total
    for p in range(parts):
        cut_ref[p] = full[:, p * piece : (p + 1) * piece].astype(bf16)


def others(axis):
    size = lax.axis_size(axis)
    me = lax.axis_index(axis)
    return [lax.rem(me + j, size) for j in range(1, size)]


def greet(axes):
    barrier = pltpu.get_barrier_semaphore()
    count = 0
    for axis in axes:
        for peer in others(axis):
            pl.semaphore_signal(barrier, inc=1, device_id={axis: peer}, device_id_type=pl.DeviceIdType.MESH)
            count += 1
    pl.semaphore_wait(barrier, count)


def push(axis, peer, src, dst, send, recv):
    return pltpu.make_async_remote_copy(
        src_ref=src, dst_ref=dst, send_sem=send.at[peer], recv_sem=recv.at[lax.axis_index(axis)],
        device_id={axis: peer}, device_id_type=pl.DeviceIdType.MESH)


def arrival(axis, peer, src, dst, send, recv):
    return pltpu.make_async_remote_copy(
        src_ref=src, dst_ref=dst, send_sem=send.at[peer], recv_sem=recv.at[peer],
        device_id={axis: peer}, device_id_type=pl.DeviceIdType.MESH)


def tokens_part(dm_ref, taps_ref, stat_ref, w_held, got_ref, feats_ref, red_ref,
                  after, dz, cut, pad, full, parts, column, rest, hop_send, hop_recv,
                  cut_send, cut_recv, st_send, st_recv, col_send, col_recv):
    me = lax.axis_index("ctx")
    size = lax.axis_size("ctx")
    mine = lax.axis_index("dp")
    hop = pltpu.make_async_remote_copy(
        src_ref=dm_ref.at[pl.ds(0, HALO)], dst_ref=after, send_sem=hop_send, recv_sem=hop_recv,
        device_id={"ctx": lax.rem(me + size - 1, size)}, device_id_type=pl.DeviceIdType.MESH)
    hop.start()
    sent = [push("ctx", p, stat_ref.at[p], parts.at[me], st_send, st_recv) for p in others("ctx")]
    for copy in sent:
        copy.start()
    hop.wait()

    @pl.when(me == size - 1)
    def _():
        after[...] = jnp.zeros(after.shape, bf16)

    dz_kernel(dm_ref, after, taps_ref, dz, cut, pad, full)
    swaps = []
    for j, p in enumerate(others("dp")):
        swaps.append(pltpu.make_async_remote_copy(
            src_ref=cut.at[p], dst_ref=got_ref.at[j + 1], send_sem=cut_send.at[j], recv_sem=cut_recv.at[j],
            device_id={"dp": p}, device_id_type=pl.DeviceIdType.MESH))
        swaps[-1].start()
    got_ref[0] = cut[mine]
    total = stat_ref[me]
    for p in others("ctx"):
        arrival("ctx", p, stat_ref.at[p], parts.at[p], st_send, st_recv).wait_recv()
        total = total + parts[p]
    column[...] = total
    spread = [push("dp", p, column, rest.at[mine], col_send, col_recv) for p in others("dp")]
    for copy in spread:
        copy.start()
    tile = 2 * LANES

    @pl.loop(0, w_held.shape[1] // tile)
    def _(i):
        at = pl.ds(pl.multiple_of(i * tile, tile), tile)
        feats_ref[:, at] = jnp.dot(dz[...], w_held[:, at], preferred_element_type=f32).astype(bf16)

    rest[mine] = column[...]
    for p in others("dp"):
        arrival("dp", p, column, rest.at[p], col_send, col_recv).wait_recv()
    total = rest[0]
    for p in range(1, rest.shape[0]):
        total = total + rest[p]
    red_ref[...] = total
    for copy in swaps:
        copy.wait()
    for copy in sent + spread:
        copy.wait_send()


def weight_part(scale, toks, got_ref, red_ref, gw_ref, taps_ref, term, pairs, land, total,
                pair_send, pair_recv, send, recv, tap_send, tap_recv):
    me = lax.axis_index("ctx")
    devices, own, _ = term.shape
    half = devices // 2
    side = lax.rem(me, 2)
    seat = me // 2
    partner = me + 1 - 2 * side
    per = 16 // math.gcd(own, 16)
    count = devices // per
    depth = got_ref.shape[0] * got_ref.shape[1]
    sent = [push("ctx", p, red_ref, taps_ref.at[me], tap_send, tap_recv) for p in others("ctx")]
    for copy in sent:
        copy.start()
    taps_ref[me] = red_ref[...]

    def handover(q, target):
        return pltpu.make_async_remote_copy(
            src_ref=term.at[target], dst_ref=pairs.at[q], send_sem=pair_send.at[q], recv_sem=pair_recv.at[q],
            device_id={"ctx": partner}, device_id_type=pl.DeviceIdType.MESH)

    def delivery(q, slot):
        return pltpu.make_async_remote_copy(
            src_ref=term.at[2 * q + side], dst_ref=land.at[slot], send_sem=send.at[q], recv_sem=recv.at[slot],
            device_id={"ctx": 2 * q + side}, device_id_type=pl.DeviceIdType.MESH)

    @pl.loop(0, count)
    def _(i):
        if per == 1:
            second = i // half
            block = 2 * lax.rem(seat + 1 + lax.rem(i, half), half) + (1 - side) + second * (2 * side - 1)
        else:
            block = i
        at = pl.ds(pl.multiple_of(block * (own * per), 16), own * per)
        rows = jnp.concatenate([toks[j, at, :] for j in range(toks.shape[0])], axis=1)
        piece = jnp.dot(rows, got_ref[...].reshape(depth, -1), preferred_element_type=f32)
        for s in range(per):
            target = block * per + s
            term[target] = piece[s * own : (s + 1) * own].astype(bf16)

            @pl.when(lax.rem(target, 2) != side)
            def _():
                handover(target // 2, target).start()

    @pl.loop(1, half)
    def _(j):
        q = lax.rem(seat + j, half)
        target = 2 * q + side
        handover(q, target).wait_recv()
        term[target] = (term[target].astype(f32) + pairs[q].astype(f32)).astype(bf16)
        delivery(q, seat).start()

    handover(seat, me).wait_recv()
    total[...] = term[me].astype(f32) + pairs[seat].astype(f32)

    @pl.loop(1, half)
    def _(j):
        q = lax.rem(seat + j, half)
        delivery(q, q).wait_recv()
        total[...] += land[q].astype(f32)

    gw_ref[...] = (total[...] * scale).astype(bf16)
    for p in others("ctx"):
        arrival("ctx", p, red_ref, taps_ref.at[p], tap_send, tap_recv).wait_recv()
    for copy in sent:
        copy.wait_send()

    @pl.loop(1, half)
    def _(j):
        q = lax.rem(seat + j, half)
        delivery(q, q).wait_send()

    @pl.loop(0, half)
    def _(q):
        handover(q, 2 * q + 1 - side).wait_send()


def shape(dims, kind=f32):
    return jax.ShapeDtypeStruct(dims, kind)


def operator_kernel(width, scale, feats_ref, taps_ref, cot_ref, modal_ref, w_ref,
                    out_ref, gf_ref, gw_ref, gt_ref, red_ref,
                    w_held, stack, toks, modal_all, rate, reff, z, zs, mixed, qkv, up, gp, eh, every,
                    inf, inb, near, filt, corr, ups, gps, first, last, dm, dm16, tap, draw, stat,
                    after, dz, cut, full, parts, column, rest, got, term, pairs, land, total, taps_all,
                    w_sem, hop_send, hop_recv, tok_send, tok_recv, mod_send, mod_recv, st_send, st_recv,
                    aft_send, aft_recv, cut_send, cut_recv, part_send, part_recv, col_send, col_recv,
                    pair_send, pair_recv, land_send, land_recv, tap_send, tap_recv):
    me = lax.axis_index("ctx")
    size = lax.axis_size("ctx")
    rows, depth = feats_ref.shape
    chans = w_held.shape[0]
    modes, wide = rate.shape
    own = width // size
    count = taps_ref.shape[0]
    cuts = [(a, min(a + 6 * LANES, chans)) for a in range(0, chans, 6 * LANES)]
    loads = [pltpu.make_async_copy(w_ref.at[a:b], w_held.at[a:b], w_sem.at[i]) for i, (a, b) in enumerate(cuts)]
    for copy in loads:
        copy.start()
    greet(["ctx", "dp"])
    hop = pltpu.make_async_remote_copy(
        src_ref=feats_ref.at[pl.ds(rows - HALO, HALO)], dst_ref=stack.at[pl.ds(0, HALO)],
        send_sem=hop_send, recv_sem=hop_recv,
        device_id={"ctx": lax.rem(me + 1, size)}, device_id_type=pl.DeviceIdType.MESH)
    hop.start()
    sent = [push("ctx", p, modal_ref, modal_all.at[me], mod_send, mod_recv) for p in others("ctx")]
    for copy in sent:
        copy.start()
    for a, b in lane_tiles(depth):
        toks[0, a:b, :] = feats_ref[:, a:b].astype(f32).T.astype(bf16)
    swaps = []
    for j, p in enumerate(others("dp")):
        swaps.append(pltpu.make_async_remote_copy(
            src_ref=toks.at[0], dst_ref=toks.at[j + 1], send_sem=tok_send.at[j], recv_sem=tok_recv.at[j],
            device_id={"dp": p}, device_id_type=pl.DeviceIdType.MESH))
        swaps[-1].start()
    stack[HALO:, :] = feats_ref[...]
    hop.wait()

    @pl.when(me == 0)
    def _():
        stack[0:HALO, :] = jnp.zeros((HALO, depth), bf16)

    for i, (a, b) in enumerate(cuts):
        loads[i].wait()
        z[:, a:b] = lax.dot_general(
            stack[...], w_held[a:b, :], (((1,), (1,)), ((), ())), preferred_element_type=f32).astype(bf16)
    modal_all[me] = modal_ref[...]
    for p in others("ctx"):
        arrival("ctx", p, modal_ref, modal_all.at[p], mod_send, mod_recv).wait_recv()
    rate[...] = jnp.zeros((modes, wide), f32)
    reff[...] = jnp.zeros((modes, wide), f32)
    for d in range(size):
        rate[:, d * own : (d + 1) * own] = modal_all[d, 0:modes]
        reff[:, d * own : (d + 1) * own] = modal_all[d, modes : 2 * modes]

    states_kernel(width, z, taps_ref, cot_ref, rate, qkv, up, gp, eh, zs, mixed)
    flow = [push("ctx", p, eh, every.at[me], st_send, st_recv) for p in others("ctx")]
    for copy in flow:
        copy.start()
    every[me] = eh[...]
    near_kernel(up, gp, rate, reff, inf, inb, near, filt, corr, ups, gps)
    for p in others("ctx"):
        arrival("ctx", p, eh, every.at[p], st_send, st_recv).wait_recv()
    join_kernel(width, me, qkv, inf, inb, near, cot_ref, rate, reff, every, zs,
                out_ref, dm16, stat, first, last, dm, tap, draw)
    tokens_part(dm16, taps_ref, stat, w_held, got, gf_ref, red_ref,
                after, dz, cut, zs, full, parts, column, rest, aft_send, aft_recv,
                cut_send, cut_recv, part_send, part_recv, col_send, col_recv)
    for copy in swaps:
        copy.wait()
    weight_part(scale, toks, got, red_ref, gw_ref, taps_all, term, pairs, land, total,
                pair_send, pair_recv, land_send, land_recv, tap_send, tap_recv)
    unit = chans // size
    for d in range(size):
        gt_ref[:, d * unit : (d + 1) * unit] = taps_all[d, 0:count, :] * scale
    for copy in sent + flow:
        copy.wait_send()


def local(tokens, w_in, conv_taps, residues, rates, cotangent):
    feats = tokens[0]
    rows, depth = feats.shape
    cot = cotangent[0]
    width = cot.shape[1]
    chans = w_in.shape[1]
    own, modes = rates.shape
    count = conv_taps.shape[0]
    ctx = lax.axis_size("ctx")
    dp = lax.axis_size("dp")
    me = lax.axis_index("ctx")
    scale = 1.0 / math.sqrt(dp * ctx * rows)
    wide = -(-width // LANES) * LANES

    amp = jnp.sqrt(-jnp.expm1(-2.0 * rates))
    modal = jnp.concatenate([rates.T, (residues * amp).T], axis=0)
    dma = pltpu.SemaphoreType.DMA
    piece = chans // dp
    own_feats = depth // ctx
    half = ctx // 2
    unit = (SUB + modes, chans // ctx)

    def held(*dims):
        return pltpu.VMEM(dims, f32)

    def short(*dims):
        return pltpu.VMEM(dims, bf16)

    scratch = [
        short(chans, depth), short(HALO + rows, depth), short(dp, depth, rows),
        held(ctx, 2 * modes, own), held(modes, wide), held(modes, wide), short(HALO + rows, chans),
        held(HALO + rows, chans), held(rows, chans), held(3, rows, wide), held(2 * rows, wide),
        held(2 * rows, wide), held(2 * modes, wide), held(ctx, 2 * modes, wide),
        held(rows, wide), held(rows, wide), held(modes, wide), held(rows, wide), held(rows, wide),
        held(SUB, 2 * rows, LANES), held(SUB, 2 * rows, LANES), held(modes, wide), held(modes, wide),
        held(rows, chans), short(rows, chans), held(count + 1, chans), held(modes, wide), held(ctx, *unit),
        short(HALO, chans), short(rows, chans), short(dp, rows, piece), held(rows, chans),
        held(ctx, *unit), held(*unit), held(dp, *unit), short(dp, rows, piece),
        short(ctx, own_feats, piece), short(half, own_feats, piece), short(half, own_feats, piece),
        held(own_feats, piece), held(ctx, *unit),
        dma((-(-chans // (6 * LANES)),)), dma, dma, dma((dp,)), dma((dp,)), dma((ctx,)), dma((ctx,)),
        dma((ctx,)), dma((ctx,)), dma, dma, dma((dp,)), dma((dp,)), dma((ctx,)), dma((ctx,)),
        dma((dp,)), dma((dp,)), dma((half,)), dma((half,)), dma((half,)), dma((half,)), dma((ctx,)), dma((ctx,)),
    ]
    output, grad_feats, grad_weight, grad_taps, red = pl.pallas_call(
        functools.partial(operator_kernel, width, scale),
        out_shape=[shape((rows, width), bf16), shape((rows, depth), bf16), shape((own_feats, piece), bf16),
                   shape((count, chans)), shape(unit)],
        in_specs=[VM] * 4 + [pl.BlockSpec(memory_space=pl.ANY)],
        out_specs=[VM] * 5,
        scratch_shapes=scratch,
        compiler_params=pltpu.CompilerParams(
            vmem_limit_bytes=56 << 20, collective_id=0, has_side_effects=True),
        cost_estimate=pl.CostEstimate(flops=10**10, bytes_accessed=1 << 24, transcendentals=0),
    )(feats, conv_taps, cot, modal, w_in.T)
    grad_residues = amp * red[SUB:, :own].T * scale
    return (output[None], grad_feats[None], grad_weight, grad_taps, grad_residues)


def solution(mesh):
    in_specs = (
        P("dp", "ctx", None),
        P(),
        P(),
        P("ctx", None),
        P("ctx", None),
        P("dp", "ctx", None),
    )
    out_specs = (P("dp", "ctx", None), P("dp", "ctx", None), P("ctx", "dp"), P(), P("ctx", None))
    return jax.shard_map(local, mesh=mesh, in_specs=in_specs, out_specs=out_specs, check_vma=False)
```
